32 devices in a mesh: dom: 8 (over y, x, core), rep: 4 (over z).
Axes of the slice: x: 2, y: 2, z: 4, core: 2. Of those that a mesh axis runs over, the one named last changes fastest.
Arguments:
- node_state: bfloat16 [32768, 256], P(('dom', 'rep')), may hold values from -6 to 6
- edge_tiles: bfloat16 [32768, 5, 128], P(('dom', 'rep')), may hold values from -0.25 to 0.25
- block_mask: int32 [256, 5], P(('dom', 'rep')), may hold values from 0 to 1, as said below
- block_len: int32 [256], P(('dom', 'rep')), may hold values from 64 to 128, as said below
- w_in: bfloat16 [512, 256], replicated, may hold values from -0.25 to 0.25
- w_out: bfloat16 [256, 256], replicated, may hold values from -0.375 to 0.375
- gain: float32 [256], replicated, may hold values from 0.5 to 1.5
- upstream: bfloat16 [32768, 256], P(('dom', 'rep')), may hold values from -6 to 6
Outputs:
- new_state: bfloat16 [32768, 256], P(('dom', 'rep'))
- grad_state: bfloat16 [32768, 256], P(('dom', 'rep'))
- grad_w_in: float32 [512, 256], replicated
- grad_w_out: float32 [256, 256], replicated
- grad_gain: float32 [256], replicated
The draws below stay inside these ranges and needn't reach their ends.
Inputs may be any that keep to these rules, and one draw needn't show every extreme that they name: `block_mask`: the block at offset 2 (a block with itself) is always coupled. `block_len`: the largest length, 128, occurs in every draw.
All inputs are finite; a program needn't handle non-finite values.
Results may differ from the reference program's by a relative error of at most 0.0058.
Values may be sent and summed in bfloat16 or wider, within the bound.
No kernel may reach another device: no remote copies, remote signals or barrier semaphores. Data moves between devices by JAX's collectives and lax.ppermute only.
A program may use at most 64 MiB of HBM per device.

```python
import math
import jax
import jax.numpy as jnp
from jax import lax

LATENT = 256
BS = 128
WBAND = 2
NOFF = 5
NB = 256
NODES = 32768


def draw_block_mask(key, part):
    key = jax.random.fold_in(key, 11)
    chosen = jax.random.randint(key, (NB, NOFF), 0, 4)
    column = lax.broadcasted_iota(jnp.int32, (NB, NOFF), 1)
    return jnp.where((chosen != 0) | (column == WBAND), 1, 0).astype(jnp.int32)


def draw_block_len(key, part):
    key = jax.random.fold_in(key, 23)
    length_key, full_key = jax.random.split(key)
    base_len = jax.random.randint(length_key, (NB,), BS // 2, BS + 1)
    full_pick = jax.random.randint(full_key, (NB,), 0, 4)
    block_index = lax.broadcasted_iota(jnp.int32, (NB,), 0)
    return jnp.where((full_pick == 0) | (block_index == 0), BS, base_len).astype(jnp.int32)


def levels(own_key, shape, cuts, low, top_value):
    level = 1.0
    for dim, shards_of in cuts:
        heights = jax.random.uniform(jax.random.fold_in(jax.random.fold_in(own_key, 6), dim), (shards_of,), jnp.float32, low / len(cuts), top_value / len(cuts))
        level = level * jnp.repeat(jnp.exp(heights), shape[dim] // shards_of).reshape((-1,) + (1,) * (len(shape) - 1 - dim))
    return level


def scatter_about(own_key, dims, scale, bound, shards=(), kind=jnp.bfloat16):
    array = jax.random.normal(own_key, dims, jnp.float32) * scale
    if len(shards) > 0:
        array = levels(own_key, dims, shards, -0.22, 0.18) * array
    return jnp.clip(array, min=-bound, max=bound).astype(kind)


def setup_inputs(seed: int = 0) -> dict:
    arg_keys = jax.random.split(jax.random.key(seed), 9)
    return {
        "node_state": scatter_about(arg_keys[0], (NODES, LATENT), 1.0, 6.0, ((0, 32),)),
        "edge_tiles": scatter_about(arg_keys[1], (NODES, NOFF, BS), (NOFF * BS) ** -0.5, 0.25, ((0, 32),)),
        "block_mask": draw_block_mask(jax.random.fold_in(arg_keys[8], 71), 0),
        "block_len": draw_block_len(jax.random.fold_in(arg_keys[8], 71), 0),
        "w_in": scatter_about(arg_keys[4], (2 * LATENT, LATENT), (2 * LATENT) ** -0.5, 0.25),
        "w_out": scatter_about(arg_keys[5], (LATENT, LATENT), LATENT ** -0.5, 0.375),
        "gain": jnp.clip(1.0 + 0.1 * jax.random.normal(arg_keys[6], (LATENT,), jnp.float32), 0.5, 1.5),
        "upstream": scatter_about(arg_keys[7], (NODES, LATENT), 1.0, 6.0, ((0, 32),)),
    }


EPSILON = 1e-05

def swish_slope(preact):
    sigma = jax.nn.sigmoid(preact)
    return sigma * (1.0 + preact * (1.0 - sigma))

def node_update(node_state, message, w_in, w_out, gain, upstream, valid_rows):
    latent = node_state.shape[1]
    joined = jnp.concatenate([node_state, message], axis=1)
    preact = jnp.dot(joined, w_in, preferred_element_type=jnp.float32)
    activated = jax.nn.silu(preact).astype(jnp.bfloat16)
    output = jnp.dot(activated, w_out, preferred_element_type=jnp.float32)
    centred = output - lax.optimization_barrier(jnp.mean(output, axis=1, keepdims=True))
    inverse = lax.rsqrt(lax.optimization_barrier(jnp.mean(centred * centred, axis=1, keepdims=True)) + EPSILON)
    normed = centred * inverse
    new_state = (node_state.astype(jnp.float32) + gain * normed * valid_rows).astype(jnp.bfloat16)
    masked_up = upstream.astype(jnp.float32) * valid_rows
    gain_terms = lax.optimization_barrier(jnp.sum(masked_up * normed, axis=0))
    scaled = masked_up * gain
    grad_output = inverse * (scaled - lax.optimization_barrier(jnp.mean(scaled, axis=1, keepdims=True)) - normed * lax.optimization_barrier(jnp.mean(scaled * normed, axis=1, keepdims=True)))
    grad_output = grad_output.astype(jnp.bfloat16)
    out_terms = jnp.dot(activated.T, grad_output, preferred_element_type=jnp.float32)
    grad_act = jnp.dot(grad_output, w_out.T, preferred_element_type=jnp.float32)
    grad_pre = (grad_act * swish_slope(preact)).astype(jnp.bfloat16)
    in_terms = jnp.dot(joined.T, grad_pre, preferred_element_type=jnp.float32)
    grad_joined = jnp.dot(grad_pre, w_in.T, preferred_element_type=jnp.float32)
    return (new_state, grad_joined[:, :latent], grad_joined[:, latent:].astype(jnp.bfloat16), in_terms, out_terms, gain_terms)

def reference(node_state, edge_tiles, block_mask, block_len, w_in, w_out, gain, upstream):
    row_count, latent = node_state.shape
    blocks = row_count // BS
    position = lax.broadcasted_iota(jnp.int32, (blocks, BS), 1)
    valid_mask = (position < block_len[:, None]).astype(jnp.float32)
    valid_rows = valid_mask.reshape(row_count, 1)
    coupling = block_mask.astype(jnp.float32)[:, None, :] * valid_mask[:, :, None]
    coupled = edge_tiles.reshape(blocks, BS, NOFF, BS) * coupling.astype(jnp.bfloat16)[..., None]
    masked = (node_state * valid_rows.astype(jnp.bfloat16)).reshape(blocks, BS, latent)
    summed = jnp.zeros((blocks, BS, latent), jnp.float32)
    for offset in range(NOFF):
        source = jnp.roll(masked, WBAND - offset, axis=0)
        summed = summed + jnp.einsum('bij,bjl->bil', coupled[:, :, offset, :].astype(jnp.float32), source.astype(jnp.float32), precision=lax.Precision.HIGHEST)
    message = summed.astype(jnp.bfloat16).reshape(row_count, latent)
    new_state, grad_direct, grad_message, in_terms, out_terms, gain_terms = node_update(node_state, message, w_in, w_out, gain, upstream, valid_rows)
    grad_blocks = grad_message.reshape(blocks, BS, latent).astype(jnp.float32)
    transposed = jnp.zeros((blocks, BS, latent), jnp.float32)
    for offset in range(NOFF):
        contrib = jnp.einsum('bij,bil->bjl', coupled[:, :, offset, :].astype(jnp.float32), grad_blocks, precision=lax.Precision.HIGHEST)
        transposed = transposed + jnp.roll(contrib, offset - WBAND, axis=0)
    transposed = transposed.reshape(row_count, latent) * valid_rows
    grad_state = (upstream.astype(jnp.float32) + grad_direct + transposed).astype(jnp.bfloat16)
    grad_scale = 1.0 / math.sqrt(NODES)
    return (new_state, grad_state, in_terms * grad_scale, out_terms * grad_scale, gain_terms * grad_scale)
```

```python
import functools
import math

import jax
import jax.numpy as jnp
from jax import lax
from jax.experimental import pallas as pl
from jax.experimental.pallas import tpu as pltpu
from jax.sharding import PartitionSpec as P

EPSILON = 1e-05
F32 = jnp.float32
BF16 = jnp.bfloat16
GAIN_ROWS = 8
VMEM_LIMIT = 40 * 1024 * 1024


def dot(a, b, contract):
    return lax.dot_general(a, b, ((contract[:1], contract[1:]), ((), ())), preferred_element_type=F32)


def local_kernel(
    cfg,
    place_ref,
    len_ref,
    mask_ref,
    state_ref,
    tiles_ref,
    up_ref,
    w_in_ref,
    w_out_ref,
    gain_ref,
    odd_ref,
    even_ref,
    new_ref,
    inner_ref,
    rim_ref,
    spill_odd_ref,
    spill_even_ref,
    send_ref,
    ext_ref,
    band_ref,
    spread_ref,
    grad_in_ref,
    grad_out_ref,
    gain_sum_ref,
):
    bs, offsets, chunks, scale = cfg
    rim = (offsets - 1) // 2 * bs
    rows, latent = state_ref.shape
    size = rows // chunks
    per = size // bs
    width = size + 2 * rim
    side = place_ref[0]
    me = place_ref[1]
    far = rows + rim

    ext_ref[pl.ds(pl.multiple_of(side * far, bs), rim), :] = odd_ref[...]
    ext_ref[pl.ds(pl.multiple_of((1 - side) * far, bs), rim), :] = even_ref[...]

    def validity(block):
        position = lax.broadcasted_iota(jnp.int32, (bs, 1), 0)
        return (position < len_ref[block]).astype(F32)

    for block in range(rows // bs):
        here = slice(block * bs, (block + 1) * bs)
        ext_ref[rim + block * bs : rim + (block + 1) * bs, :] = (
            state_ref[here, :].astype(F32) * validity(block)
        ).astype(BF16)

    spread_ref[...] = jnp.zeros_like(spread_ref)
    grad_in_ref[...] = jnp.zeros_like(grad_in_ref)
    grad_out_ref[...] = jnp.zeros_like(grad_out_ref)
    gain_sum_ref[...] = jnp.zeros_like(gain_sum_ref)
    gain = gain_ref[...]

    for chunk in range(chunks):
        first = chunk * per
        here = slice(chunk * size, (chunk + 1) * size)
        valid = jnp.concatenate([validity(first + j) for j in range(per)], axis=0)
        for j in range(per):
            row = slice(j * bs, (j + 1) * bs)
            for column in range(width // bs):
                offset = column - j
                cols = slice(column * bs, (column + 1) * bs)
                if 0 <= offset < offsets:
                    tile = tiles_ref[offset, (first + j) * bs : (first + j + 1) * bs, :]
                    on = mask_ref[first + j, offset].astype(F32).astype(BF16)
                    band_ref[row, cols] = tile * on
                else:
                    band_ref[row, cols] = jnp.zeros((bs, bs), BF16)
        band = band_ref[...]
        reach = slice(chunk * size, chunk * size + width)
        message = (dot(band, ext_ref[reach, :], (1, 0)) * valid).astype(BF16)
        state = state_ref[here, :]
        preact = dot(state, w_in_ref[:latent, :], (1, 0)) + dot(message, w_in_ref[latent:, :], (1, 0))
        sigma = jax.nn.sigmoid(preact)
        activated = (preact * sigma).astype(BF16)
        output = dot(activated, w_out_ref[...], (1, 0))
        centred = output - jnp.mean(output, axis=1, keepdims=True)
        inverse = lax.rsqrt(jnp.mean(centred * centred, axis=1, keepdims=True) + EPSILON)
        normed = centred * inverse
        new_ref[here, :] = (state.astype(F32) + gain * normed * valid).astype(BF16)
        upstream = up_ref[here, :].astype(F32)
        masked_up = upstream * valid
        gain_sum_ref[...] += jnp.sum(masked_up * normed, axis=0, keepdims=True)
        scaled = masked_up * gain
        grad_output = (
            inverse
            * (
                scaled
                - jnp.mean(scaled, axis=1, keepdims=True)
                - normed * jnp.mean(scaled * normed, axis=1, keepdims=True)
            )
        ).astype(BF16)
        grad_out_ref[...] += dot(activated, grad_output, (0, 0))
        grad_act = dot(grad_output, w_out_ref[...], (1, 1))
        slope = sigma * (1.0 + preact * (1.0 - sigma))
        grad_pre = (grad_act * slope).astype(BF16)
        grad_in_ref[:latent, :] += dot(state, grad_pre, (0, 0))
        grad_in_ref[latent:, :] += dot(message, grad_pre, (0, 0))
        direct = dot(grad_pre, w_in_ref[:latent, :], (1, 1))
        grad_message = dot(grad_pre, w_in_ref[latent:, :], (1, 1)).astype(BF16)
        grad_message = (grad_message.astype(F32) * valid).astype(BF16)
        spread_ref[reach, :] += dot(band, grad_message, (0, 0))
        own = upstream + direct
        if chunk == 0:
            rim_ref[:size, :] = own
        elif chunk == chunks - 1:
            rim_ref[size:, :] = own
        else:
            inner_ref[here, :] = own

    for block in range(rows // bs):
        here = slice(block * bs, (block + 1) * bs)
        back = spread_ref[rim + block * bs : rim + (block + 1) * bs, :] * validity(block)
        if block < per:
            rim_ref[here, :] += back
        elif block >= rows // bs - per:
            there = slice(size - rows + here.start + size, size - rows + here.stop + size)
            rim_ref[there, :] += back
        else:
            inner_ref[here, :] += back
    spill_odd_ref[...] = spread_ref[pl.ds(pl.multiple_of(side * far, bs), rim), :].astype(BF16)
    spill_even_ref[...] = spread_ref[pl.ds(pl.multiple_of((1 - side) * far, bs), rim), :].astype(BF16)

    count = send_ref.shape[0] * send_ref.shape[1]
    n_in = grad_in_ref.shape[0] // count
    n_out = grad_out_ref.shape[0] // count
    top = lax.broadcasted_iota(jnp.int32, (GAIN_ROWS, latent), 0) == 0
    for piece in range(count):
        turn = lax.bitwise_xor(me, piece)
        half = lax.bitwise_and(turn, 1)
        slot = lax.shift_right_logical(turn, 1)
        send_ref[half, slot, :n_in, :] = (grad_in_ref[piece * n_in : (piece + 1) * n_in, :] * scale).astype(BF16)
        send_ref[half, slot, n_in : n_in + n_out, :] = (
            grad_out_ref[piece * n_out : (piece + 1) * n_out, :] * scale
        ).astype(BF16)
        if piece == 0:
            tail = jnp.where(top, gain_sum_ref[...] * scale, 0.0)
        else:
            tail = jnp.zeros((GAIN_ROWS, latent), F32)
        send_ref[half, slot, n_in + n_out :, :] = tail.astype(BF16)


def finish_kernel(bs, place_ref, len_ref, inner_ref, rim_ref, odd_ref, even_ref, out_ref, held_ref):
    rows = inner_ref.shape[0]
    size = odd_ref.shape[0]
    side = place_ref[0]
    held_ref[pl.ds(pl.multiple_of(side * size, bs), size), :] = odd_ref[...]
    held_ref[pl.ds(pl.multiple_of((1 - side) * size, bs), size), :] = even_ref[...]
    blocks = rows // bs
    per = size // bs
    position = lax.broadcasted_iota(jnp.int32, (bs, 1), 0)
    for block in range(blocks):
        here = slice(block * bs, (block + 1) * bs)
        if block < per:
            there = here
        elif block >= blocks - per:
            there = slice(2 * size - rows + here.start, 2 * size - rows + here.stop)
        else:
            out_ref[here, :] = inner_ref[here, :].astype(BF16)
            continue
        valid = (position < len_ref[block]).astype(F32)
        out_ref[here, :] = (rim_ref[there, :] + held_ref[there, :].astype(F32) * valid).astype(BF16)


def unpack_kernel(place_ref, near_ref, far_ref, grad_in_ref, grad_out_ref, gain_ref):
    me = place_ref[1]
    count = 2 * near_ref.shape[0]
    n_in = grad_in_ref.shape[0] // count
    n_out = grad_out_ref.shape[0] // count
    for turn in range(count):
        source = (far_ref if turn % 2 else near_ref).at[turn // 2]
        piece = lax.bitwise_xor(me, turn)
        at_in = pl.ds(pl.multiple_of(piece * n_in, n_in), n_in)
        at_out = pl.ds(pl.multiple_of(piece * n_out, n_out), n_out)
        grad_in_ref[at_in, :] = source[:n_in, :].astype(F32)
        grad_out_ref[at_out, :] = source[n_in : n_in + n_out, :].astype(F32)

        @pl.when(piece == 0)
        def _():
            gain_ref[...] = source[n_in + n_out :, :].astype(F32)[:1, :]


def swap(x, axis, turn):
    count = lax.axis_size(axis)
    return lax.ppermute(x, axis, [(i, i ^ turn) for i in range(count)])


def whole_sum(x, axis):
    count = lax.axis_size(axis)
    if count & (count - 1) == 0:
        parts = [x.astype(F32)] + [swap(x, axis, k).astype(F32) for k in range(1, count)]
        while len(parts) > 1:
            parts = [parts[i] + parts[i + 1] for i in range(0, len(parts), 2)]
        return parts[0].astype(x.dtype)
    moved = [x] + [
        lax.ppermute(x, axis, [(i, (i + k) % count) for i in range(count)]) for k in range(1, count)
    ]
    order = (lax.axis_index(axis) - jnp.arange(count)) % count
    stacked = jnp.stack(moved)[order]
    return jnp.sum(stacked.astype(F32), axis=0).astype(x.dtype)


def vmem(count):
    return [pl.BlockSpec(memory_space=pltpu.VMEM)] * count


def smem(count):
    return [pl.BlockSpec(memory_space=pltpu.SMEM)] * count


def local(node_state, edge_tiles, block_mask, block_len, w_in, w_out, gain, upstream):
    rows, latent = node_state.shape
    offsets, bs = edge_tiles.shape[1:]
    blocks = rows // bs
    rim = (offsets - 1) // 2 * bs
    size = rim
    chunks = rows // size
    dom = lax.axis_size("dom")
    rep = lax.axis_size("rep")
    total = dom * rep
    me = lax.axis_index("dom")
    side = (me * rep + lax.axis_index("rep")) % 2
    place = jnp.stack([side, me]).astype(jnp.int32)
    scale = 1.0 / math.sqrt(rows * total)
    ring = ("dom", "rep")
    even_pairs = [(i, i ^ 1) for i in range(total)]
    odd_pairs = [(i, (i + 1) % total if i % 2 else (i - 1) % total) for i in range(total)]

    position = lax.broadcasted_iota(jnp.int32, (blocks, bs), 1)
    valid = (position < block_len[:, None]).astype(BF16).reshape(rows, 1)
    masked = node_state * valid
    low, high = masked[:rim], masked[rows - rim :]
    to_odd = jnp.where(side == 0, low, high)
    to_even = jnp.where(side == 0, high, low)
    from_even = lax.ppermute(to_even, ring, even_pairs)
    from_odd = lax.ppermute(to_odd, ring, odd_pairs)

    tiles = jnp.transpose(edge_tiles, (1, 0, 2))
    n_in, n_out = w_in.shape[0] // dom, w_out.shape[0] // dom
    piece_rows = n_in + n_out + GAIN_ROWS
    params = pltpu.CompilerParams(vmem_limit_bytes=VMEM_LIMIT)
    new_state, inner, outer, spill_odd, spill_even, send = pl.pallas_call(
        functools.partial(local_kernel, (bs, offsets, chunks, scale)),
        out_shape=(
            jax.ShapeDtypeStruct((rows, latent), BF16),
            jax.ShapeDtypeStruct((rows, latent), F32),
            jax.ShapeDtypeStruct((2 * size, latent), F32),
            jax.ShapeDtypeStruct((rim, latent), BF16),
            jax.ShapeDtypeStruct((rim, latent), BF16),
            jax.ShapeDtypeStruct((2, dom // 2, piece_rows, latent), BF16),
        ),
        in_specs=smem(3) + vmem(8),
        out_specs=tuple(vmem(6)),
        scratch_shapes=[
            pltpu.VMEM((rows + 2 * rim, latent), BF16),
            pltpu.VMEM((size, size + 2 * rim), BF16),
            pltpu.VMEM((rows + 2 * rim, latent), F32),
            pltpu.VMEM(w_in.shape, F32),
            pltpu.VMEM(w_out.shape, F32),
            pltpu.VMEM((1, latent), F32),
        ],
        compiler_params=params,
        name="node_update",
    )(place, block_len, block_mask, node_state, tiles, upstream, w_in, w_out, gain.reshape(1, latent), from_odd, from_even)

    back_even = lax.ppermute(spill_even, ring, even_pairs)
    back_odd = lax.ppermute(spill_odd, ring, odd_pairs)
    grad_state = pl.pallas_call(
        functools.partial(finish_kernel, bs),
        out_shape=jax.ShapeDtypeStruct((rows, latent), BF16),
        in_specs=smem(2) + vmem(4),
        out_specs=vmem(1)[0],
        scratch_shapes=[pltpu.VMEM((2 * size, latent), BF16)],
        compiler_params=params,
        name="finish_state",
    )(place, block_len, inner, outer, back_odd, back_even)

    held = (send[0].astype(F32) + swap(send[1], "dom", 1).astype(F32)).astype(BF16)
    quarter = held[0].astype(F32)
    for k in range(1, dom // 2):
        quarter = quarter + swap(held[k], "dom", 2 * k).astype(F32)
    mine = whole_sum(quarter.astype(BF16), "rep")
    near = jnp.stack([mine] + [swap(mine, "dom", 2 * k) for k in range(1, dom // 2)])
    other = swap(near, "dom", 1)
    grad_w_in, grad_w_out, grad_gain = pl.pallas_call(
        unpack_kernel,
        out_shape=(
            jax.ShapeDtypeStruct(w_in.shape, F32),
            jax.ShapeDtypeStruct(w_out.shape, F32),
            jax.ShapeDtypeStruct((1, latent), F32),
        ),
        in_specs=smem(1) + vmem(2),
        out_specs=tuple(vmem(3)),
        compiler_params=params,
        name="unpack_sums",
    )(place, near, other)
    return new_state, grad_state, grad_w_in, grad_w_out, grad_gain.reshape(latent)


def solution(mesh):
    placed = (
        P(("dom", "rep"), None),
        P(("dom", "rep"), None, None),
        P(("dom", "rep"), None),
        P(("dom", "rep")),
        P(),
        P(),
        P(),
        P(("dom", "rep"), None),
    )
    return jax.shard_map(
        local,
        mesh=mesh,
        in_specs=placed,
        out_specs=(P(("dom", "rep"), None), P(("dom", "rep"), None), P(), P(), P()),
        check_vma=False,
    )
```

```python
import functools
import math

import jax
import jax.numpy as jnp
from jax import lax
from jax.experimental import pallas as pl
from jax.experimental.pallas import tpu as pltpu
from jax.sharding import PartitionSpec as P

EPSILON = 1e-05
F32 = jnp.float32
BF16 = jnp.bfloat16
GAIN_ROWS = 8
VMEM_LIMIT = 40 * 1024 * 1024


def dot(a, b, contract):
    return lax.dot_general(a, b, ((contract[:1], contract[1:]), ((), ())), preferred_element_type=F32)


def sublane(bs):
    return lax.broadcasted_iota(jnp.int32, (bs, 1), 0)


def validity(len_ref, first, count, bs):
    return jnp.concatenate(
        [(sublane(bs) < len_ref[first + j]).astype(F32) for j in range(count)], axis=0
    )


def pack_kernel(bs, place_ref, len_ref, state_ref, odd_ref, even_ref, held_ref, sems):
    rows = state_ref.shape[0]
    rim = odd_ref.shape[0]
    per = rim // bs
    low = pltpu.make_async_copy(state_ref.at[pl.ds(0, rim), :], held_ref.at[0], sems.at[0])
    high = pltpu.make_async_copy(state_ref.at[pl.ds(rows - rim, rim), :], held_ref.at[1], sems.at[1])
    low.start()
    high.start()
    side = place_ref[0]
    low.wait()
    high.wait()
    blocks = rows // bs
    for j in range(per):
        here = slice(j * bs, (j + 1) * bs)
        top = held_ref[0, here, :] * (sublane(bs) < len_ref[j]).astype(F32).astype(BF16)
        end = held_ref[1, here, :] * (sublane(bs) < len_ref[blocks - per + j]).astype(F32).astype(BF16)
        odd_ref[here, :] = jnp.where(side == 0, top, end)
        even_ref[here, :] = jnp.where(side == 0, end, top)


def fill_band(band_ref, tiles_ref, mask_ref, first, per, bs, offsets):
    for j in range(per):
        row = slice(j * bs, (j + 1) * bs)
        for column in range(per + offsets - 1):
            offset = column - j
            cols = slice(column * bs, (column + 1) * bs)
            if 0 <= offset < offsets:
                tile = tiles_ref[offset, (first + j) * bs : (first + j + 1) * bs, :]
                band_ref[row, cols] = tile * mask_ref[first + j, offset].astype(F32).astype(BF16)
            else:
                band_ref[row, cols] = jnp.zeros((bs, bs), BF16)


def node_rows(state, message, direct_part, upstream, valid, w_in_ref, w_out_ref, gain):
    latent = state.shape[1]
    preact = direct_part + dot(message, w_in_ref[latent:, :], (1, 0))
    sigma = jax.nn.sigmoid(preact)
    activated = (preact * sigma).astype(BF16)
    output = dot(activated, w_out_ref[...], (1, 0))
    centred = output - jnp.mean(output, axis=1, keepdims=True)
    inverse = lax.rsqrt(jnp.mean(centred * centred, axis=1, keepdims=True) + EPSILON)
    normed = centred * inverse
    new_state = (state.astype(F32) + gain * normed * valid).astype(BF16)
    masked_up = upstream * valid
    gain_sum = jnp.sum(masked_up * normed, axis=0, keepdims=True)
    scaled = masked_up * gain
    grad_output = (
        inverse
        * (
            scaled
            - jnp.mean(scaled, axis=1, keepdims=True)
            - normed * jnp.mean(scaled * normed, axis=1, keepdims=True)
        )
    ).astype(BF16)
    grad_act = dot(grad_output, w_out_ref[...], (1, 1))
    slope = sigma * (1.0 + preact * (1.0 - sigma))
    grad_pre = (grad_act * slope).astype(BF16)
    return new_state, gain_sum, activated, grad_output, grad_pre


def inner_kernel(
    cfg,
    len_ref,
    mask_ref,
    state_ref,
    tiles_ref,
    up_ref,
    w_in_ref,
    w_out_ref,
    gain_ref,
    new_ref,
    own_ref,
    spread_ref,
    grad_in_ref,
    grad_out_ref,
    gain_sum_ref,
    rim_band_ref,
    rim_message_ref,
    rim_direct_ref,
    ext_ref,
    band_ref,
):
    bs, offsets = cfg
    rim = (offsets - 1) // 2 * bs
    rows, latent = state_ref.shape
    per = rim // bs
    blocks = rows // bs
    inside = rows - 2 * rim
    width = 3 * rim

    ext_ref[...] = (state_ref[...].astype(F32) * validity(len_ref, 0, blocks, bs)).astype(BF16)
    message = []
    for chunk in range(1, rows // rim - 1):
        band = band_ref.at[chunk - 1]
        fill_band(band, tiles_ref, mask_ref, chunk * per, per, bs, offsets)
        message.append(dot(band[...], ext_ref[(chunk - 1) * rim : (chunk - 1) * rim + width, :], (1, 0)))
    inner = slice(rim, rows - rim)
    valid = validity(len_ref, per, blocks - 2 * per, bs)
    message = (jnp.concatenate(message, axis=0) * valid).astype(BF16)
    state = state_ref[inner, :]
    upstream = up_ref[inner, :].astype(F32)
    direct_part = dot(state, w_in_ref[:latent, :], (1, 0))
    new_state, gain_sum, activated, grad_output, grad_pre = node_rows(
        state, message, direct_part, upstream, valid, w_in_ref, w_out_ref, gain_ref[...]
    )
    new_ref[...] = new_state
    gain_sum_ref[...] = gain_sum
    grad_out_ref[...] = dot(activated, grad_output, (0, 0))
    grad_in_ref[:latent, :] = dot(state, grad_pre, (0, 0))
    grad_in_ref[latent:, :] = dot(message, grad_pre, (0, 0))
    own_ref[...] = upstream + dot(grad_pre, w_in_ref[:latent, :], (1, 1))
    grad_message = dot(grad_pre, w_in_ref[latent:, :], (1, 1)).astype(BF16)
    grad_message = (grad_message.astype(F32) * valid).astype(BF16)
    spread_ref[...] = jnp.zeros_like(spread_ref)
    for chunk in range(1, rows // rim - 1):
        reach = slice((chunk - 1) * rim, (chunk - 1) * rim + width)
        spread_ref[reach, :] += dot(
            band_ref[chunk - 1], grad_message[(chunk - 1) * rim : chunk * rim, :], (0, 0)
        )

    for end in range(2):
        first = end * (blocks - per)
        band = rim_band_ref.at[end]
        fill_band(band, tiles_ref, mask_ref, first, per, bs, offsets)
        here = slice(end * rim, (end + 1) * rim)
        if end == 0:
            rim_message_ref[here, :] = dot(band[:, rim:], ext_ref[: 2 * rim, :], (1, 0))
        else:
            rim_message_ref[here, :] = dot(band[:, : 2 * rim], ext_ref[rows - 2 * rim :, :], (1, 0))
        rim_direct_ref[here, :] = dot(
            state_ref[first * bs : first * bs + rim, :], w_in_ref[:latent, :], (1, 0)
        )


def rim_kernel(
    cfg,
    place_ref,
    len_ref,
    state_ref,
    up_ref,
    w_in_ref,
    w_out_ref,
    gain_ref,
    band_ref,
    message_ref,
    direct_ref,
    inner_in_ref,
    inner_out_ref,
    inner_gain_ref,
    odd_ref,
    even_ref,
    send_ref,
    spill_odd_ref,
    spill_even_ref,
    new_ref,
    own_ref,
    spread_ref,
    grad_in_ref,
    grad_out_ref,
):
    bs, scale = cfg
    rows, latent = state_ref.shape
    rim = odd_ref.shape[0]
    per = rim // bs
    blocks = rows // bs
    side = place_ref[0]
    me = place_ref[1]
    odd = odd_ref[...]
    even = even_ref[...]
    low = jnp.where(side == 0, odd, even)
    high = jnp.where(side == 0, even, odd)
    valid = jnp.concatenate(
        [validity(len_ref, 0, per, bs), validity(len_ref, blocks - per, per, bs)], axis=0
    )
    arrived = jnp.concatenate(
        [dot(band_ref[0, :, :rim], low, (1, 0)), dot(band_ref[1, :, 2 * rim :], high, (1, 0))], axis=0
    )
    message = ((message_ref[...] + arrived) * valid).astype(BF16)
    state = jnp.concatenate([state_ref[:rim, :], state_ref[rows - rim :, :]], axis=0)
    upstream = jnp.concatenate([up_ref[:rim, :], up_ref[rows - rim :, :]], axis=0).astype(F32)
    new_state, gain_sum, activated, grad_output, grad_pre = node_rows(
        state, message, direct_ref[...], upstream, valid, w_in_ref, w_out_ref, gain_ref[...]
    )
    new_ref[...] = new_state
    gain_sum = gain_sum + inner_gain_ref[...]
    grad_out_ref[...] = inner_out_ref[...] + dot(activated, grad_output, (0, 0))
    grad_in_ref[:latent, :] = inner_in_ref[:latent, :] + dot(state, grad_pre, (0, 0))
    grad_in_ref[latent:, :] = inner_in_ref[latent:, :] + dot(message, grad_pre, (0, 0))
    own_ref[...] = upstream + dot(grad_pre, w_in_ref[:latent, :], (1, 1))
    grad_message = dot(grad_pre, w_in_ref[latent:, :], (1, 1)).astype(BF16)
    grad_message = (grad_message.astype(F32) * valid).astype(BF16)
    left = dot(band_ref[0], grad_message[:rim, :], (0, 0))
    right = dot(band_ref[1], grad_message[rim:, :], (0, 0))
    spread_ref[: 2 * rim, :] = left[rim:, :]
    spread_ref[2 * rim :, :] = right[: 2 * rim, :]
    low = left[:rim, :].astype(BF16)
    high = right[2 * rim :, :].astype(BF16)
    spill_odd_ref[...] = jnp.where(side == 0, low, high)
    spill_even_ref[...] = jnp.where(side == 0, high, low)

    count = send_ref.shape[0] * send_ref.shape[1]
    n_in = grad_in_ref.shape[0] // count
    n_out = grad_out_ref.shape[0] // count
    top = lax.broadcasted_iota(jnp.int32, (GAIN_ROWS, latent), 0) == 0
    for piece in range(count):
        turn = lax.bitwise_xor(me, piece)
        half = lax.bitwise_and(turn, 1)
        slot = lax.shift_right_logical(turn, 1)
        send_ref[half, slot, :n_in, :] = (grad_in_ref[piece * n_in : (piece + 1) * n_in, :] * scale).astype(BF16)
        send_ref[half, slot, n_in : n_in + n_out, :] = (
            grad_out_ref[piece * n_out : (piece + 1) * n_out, :] * scale
        ).astype(BF16)
        if piece == 0:
            tail = jnp.where(top, gain_sum * scale, 0.0)
        else:
            tail = jnp.zeros((GAIN_ROWS, latent), F32)
        send_ref[half, slot, n_in + n_out :, :] = tail.astype(BF16)


def finish_kernel(
    bs,
    place_ref,
    len_ref,
    new_inner_ref,
    new_rim_ref,
    own_inner_ref,
    own_rim_ref,
    spread_inner_ref,
    spread_rim_ref,
    odd_ref,
    even_ref,
    new_ref,
    out_ref,
):
    rows = out_ref.shape[0]
    rim = odd_ref.shape[0]
    per = rim // bs
    blocks = rows // bs
    side = place_ref[0]
    odd = odd_ref[...].astype(F32)
    even = even_ref[...].astype(F32)
    new_ref[:rim, :] = new_rim_ref[:rim, :]
    new_ref[rim : rows - rim, :] = new_inner_ref[...]
    new_ref[rows - rim :, :] = new_rim_ref[rim:, :]
    inner = slice(rim, rows - rim)
    out_ref[inner, :] = (
        own_inner_ref[...]
        + (spread_inner_ref[inner, :] + spread_rim_ref[inner, :])
        * validity(len_ref, per, blocks - 2 * per, bs)
    ).astype(BF16)
    for end in range(2):
        first = end * (blocks - per)
        here = slice(first * bs, first * bs + rim)
        there = slice(end * rim, (end + 1) * rim)
        back = jnp.where(side == end, odd, even)
        out_ref[here, :] = (
            own_rim_ref[there, :]
            + (spread_inner_ref[here, :] + spread_rim_ref[here, :] + back)
            * validity(len_ref, first, per, bs)
        ).astype(BF16)


def unpack_kernel(place_ref, near_ref, far_ref, grad_in_ref, grad_out_ref, gain_ref):
    me = place_ref[1]
    count = 2 * near_ref.shape[0]
    n_in = grad_in_ref.shape[0] // count
    n_out = grad_out_ref.shape[0] // count
    for turn in range(count):
        source = (far_ref if turn % 2 else near_ref).at[turn // 2]
        piece = lax.bitwise_xor(me, turn)
        at_in = pl.ds(pl.multiple_of(piece * n_in, n_in), n_in)
        at_out = pl.ds(pl.multiple_of(piece * n_out, n_out), n_out)
        grad_in_ref[at_in, :] = source[:n_in, :].astype(F32)
        grad_out_ref[at_out, :] = source[n_in : n_in + n_out, :].astype(F32)

        @pl.when(piece == 0)
        def _():
            gain_ref[...] = source[n_in + n_out :, :].astype(F32)[:1, :]


def swap(x, axis, turn):
    count = lax.axis_size(axis)
    return lax.ppermute(x, axis, [(i, i ^ turn) for i in range(count)])


def whole_sum(x, axis):
    count = lax.axis_size(axis)
    if count & (count - 1) == 0:
        parts = [x.astype(F32)] + [swap(x, axis, k).astype(F32) for k in range(1, count)]
        while len(parts) > 1:
            parts = [parts[i] + parts[i + 1] for i in range(0, len(parts), 2)]
        return parts[0].astype(x.dtype)
    moved = [x] + [
        lax.ppermute(x, axis, [(i, (i + k) % count) for i in range(count)]) for k in range(1, count)
    ]
    order = (lax.axis_index(axis) - jnp.arange(count)) % count
    stacked = jnp.stack(moved)[order]
    return jnp.sum(stacked.astype(F32), axis=0).astype(x.dtype)


def vmem(count):
    return [pl.BlockSpec(memory_space=pltpu.VMEM)] * count


def smem(count):
    return [pl.BlockSpec(memory_space=pltpu.SMEM)] * count


def shapes(*given):
    return tuple(jax.ShapeDtypeStruct(shape, dtype) for shape, dtype in given)


def kernel(body, name, inputs, outputs, scratch=(), flops=0, moved=0):
    scalars, arrays, anywhere = inputs
    return pl.pallas_call(
        body,
        out_shape=outputs,
        in_specs=smem(scalars) + [pl.BlockSpec(memory_space=pl.ANY)] * anywhere + vmem(arrays),
        out_specs=tuple(vmem(len(outputs))),
        scratch_shapes=list(scratch),
        compiler_params=pltpu.CompilerParams(vmem_limit_bytes=VMEM_LIMIT),
        cost_estimate=pl.CostEstimate(flops=flops, bytes_accessed=moved, transcendentals=0),
        name=name,
    )


def local(node_state, edge_tiles, block_mask, block_len, w_in, w_out, gain, upstream):
    rows, latent = node_state.shape
    offsets, bs = edge_tiles.shape[1:]
    rim = (offsets - 1) // 2 * bs
    inside = rows - 2 * rim
    width = 3 * rim
    dom = lax.axis_size("dom")
    rep = lax.axis_size("rep")
    total = dom * rep
    me = lax.axis_index("dom")
    side = (me * rep + lax.axis_index("rep")) % 2
    place = jnp.stack([side, me]).astype(jnp.int32)
    scale = 1.0 / math.sqrt(rows * total)
    ring = ("dom", "rep")
    even_pairs = [(i, i ^ 1) for i in range(total)]
    odd_pairs = [(i, (i + 1) % total if i % 2 else (i - 1) % total) for i in range(total)]
    gain_row = gain.reshape(1, latent)
    tiles = jnp.transpose(edge_tiles, (1, 0, 2))

    to_odd, to_even = kernel(
        functools.partial(pack_kernel, bs),
        "pack_rims",
        (2, 0, 1),
        shapes(((rim, latent), BF16), ((rim, latent), BF16)),
        [pltpu.VMEM((2, rim, latent), BF16), pltpu.SemaphoreType.DMA((2,))],
    )(place, block_len, node_state)
    from_odd = lax.ppermute(to_odd, ring, odd_pairs)
    from_even = lax.ppermute(to_even, ring, even_pairs)

    work = 2 * inside * latent * (width + 5 * latent + 2 * latent + 2 * latent + width)
    new_inner, own_inner, spread_inner, sum_in, sum_out, sum_gain, band, message, direct = kernel(
        functools.partial(inner_kernel, (bs, offsets)),
        "inner_rows",
        (2, 6, 0),
        shapes(
            ((inside, latent), BF16),
            ((inside, latent), F32),
            ((rows, latent), F32),
            (w_in.shape, F32),
            (w_out.shape, F32),
            ((1, latent), F32),
            ((2, rim, width), BF16),
            ((2 * rim, latent), F32),
            ((2 * rim, latent), F32),
        ),
        [pltpu.VMEM((rows, latent), BF16), pltpu.VMEM((inside // rim, rim, width), BF16)],
        flops=work,
        moved=10 * 1024 * 1024,
    )(block_len, block_mask, node_state, tiles, upstream, w_in, w_out, gain_row)

    n_in, n_out = w_in.shape[0] // dom, w_out.shape[0] // dom
    piece_rows = n_in + n_out + GAIN_ROWS
    send, spill_odd, spill_even, new_rim, own_rim, spread_rim = kernel(
        functools.partial(rim_kernel, (bs, scale)),
        "rim_rows",
        (2, 13, 0),
        shapes(
            ((2, dom // 2, piece_rows, latent), BF16),
            ((rim, latent), BF16),
            ((rim, latent), BF16),
            ((2 * rim, latent), BF16),
            ((2 * rim, latent), F32),
            ((rows, latent), F32),
        ),
        [pltpu.VMEM(w_in.shape, F32), pltpu.VMEM(w_out.shape, F32)],
        flops=work,
        moved=8 * 1024 * 1024,
    )(
        place, block_len, node_state, upstream, w_in, w_out, gain_row,
        band, message, direct, sum_in, sum_out, sum_gain, from_odd, from_even,
    )

    back_odd = lax.ppermute(spill_odd, ring, odd_pairs)
    back_even = lax.ppermute(spill_even, ring, even_pairs)
    new_state, grad_state = kernel(
        functools.partial(finish_kernel, bs),
        "finish_state",
        (2, 8, 0),
        shapes(((rows, latent), BF16), ((rows, latent), BF16)),
    )(place, block_len, new_inner, new_rim, own_inner, own_rim, spread_inner, spread_rim, back_odd, back_even)

    held = (send[0].astype(F32) + swap(send[1], "dom", 1).astype(F32)).astype(BF16)
    quarter = held[0].astype(F32)
    for k in range(1, dom // 2):
        quarter = quarter + swap(held[k], "dom", 2 * k).astype(F32)
    mine = whole_sum(quarter.astype(BF16), "rep")
    mine, grad_state, new_state = lax.optimization_barrier((mine, grad_state, new_state))
    near = jnp.stack([mine] + [swap(mine, "dom", 2 * k) for k in range(1, dom // 2)])
    other = swap(near, "dom", 1)
    grad_w_in, grad_w_out, grad_gain = kernel(
        unpack_kernel,
        "unpack_sums",
        (1, 2, 0),
        shapes((w_in.shape, F32), (w_out.shape, F32), ((1, latent), F32)),
    )(place, near, other)
    return new_state, grad_state, grad_w_in, grad_w_out, grad_gain.reshape(latent)


def solution(mesh):
    placed = (
        P(("dom", "rep"), None),
        P(("dom", "rep"), None, None),
        P(("dom", "rep"), None),
        P(("dom", "rep")),
        P(),
        P(),
        P(),
        P(("dom", "rep"), None),
    )
    return jax.shard_map(
        local,
        mesh=mesh,
        in_specs=placed,
        out_specs=(P(("dom", "rep"), None), P(("dom", "rep"), None), P(), P(), P()),
        check_vma=False,
    )
```

```python
import functools
import math

import jax
import jax.numpy as jnp
from jax import lax
from jax.experimental import pallas as pl
from jax.experimental.pallas import tpu as pltpu
from jax.sharding import PartitionSpec as P

EPSILON = 1e-05
F32 = jnp.float32
BF16 = jnp.bfloat16
GAIN_ROWS = 8
VMEM_LIMIT = 40 * 1024 * 1024


def dot(a, b, contract):
    return lax.dot_general(a, b, ((contract[:1], contract[1:]), ((), ())), preferred_element_type=F32)


def sublane(bs):
    return lax.broadcasted_iota(jnp.int32, (bs, 1), 0)


def validity(len_ref, first, count, bs):
    return jnp.concatenate(
        [(sublane(bs) < len_ref[first + j]).astype(F32) for j in range(count)], axis=0
    )


def place():
    me = lax.axis_index("dom")
    index = me * lax.axis_size("rep") + lax.axis_index("rep")
    return lax.rem(index, 2), me


def pack_kernel(bs, len_ref, state_ref, odd_ref, even_ref, held_ref, lens_ref, sems):
    rows = state_ref.shape[0]
    rim = odd_ref.shape[0]
    per = rim // bs
    copies = [
        pltpu.make_async_copy(len_ref, lens_ref, sems.at[0]),
        pltpu.make_async_copy(state_ref.at[pl.ds(0, rim), :], held_ref.at[0], sems.at[1]),
        pltpu.make_async_copy(state_ref.at[pl.ds(rows - rim, rim), :], held_ref.at[1], sems.at[2]),
    ]
    for copy in copies:
        copy.start()
    side, _ = place()
    for copy in copies:
        copy.wait()
    blocks = rows // bs
    for j in range(per):
        here = slice(j * bs, (j + 1) * bs)
        top = held_ref[0, here, :] * (sublane(bs) < lens_ref[j]).astype(F32).astype(BF16)
        end = held_ref[1, here, :] * (sublane(bs) < lens_ref[blocks - per + j]).astype(F32).astype(BF16)
        odd_ref[here, :] = jnp.where(side == 0, top, end)
        even_ref[here, :] = jnp.where(side == 0, end, top)


def fill_band(band_ref, tiles_ref, mask_ref, first, per, bs, offsets):
    for j in range(per):
        row = slice(j * bs, (j + 1) * bs)
        for column in range(per + offsets - 1):
            offset = column - j
            cols = slice(column * bs, (column + 1) * bs)
            if 0 <= offset < offsets:
                tile = tiles_ref[offset, (first + j) * bs : (first + j + 1) * bs, :]
                band_ref[row, cols] = tile * mask_ref[first + j, offset].astype(F32).astype(BF16)
            else:
                band_ref[row, cols] = jnp.zeros((bs, bs), BF16)


def node_rows(state, message, direct_part, upstream, valid, w_in_ref, w_out_ref, gain):
    latent = state.shape[1]
    preact = direct_part + dot(message, w_in_ref[latent:, :], (1, 0))
    sigma = jax.nn.sigmoid(preact)
    activated = (preact * sigma).astype(BF16)
    output = dot(activated, w_out_ref[...], (1, 0))
    centred = output - jnp.mean(output, axis=1, keepdims=True)
    inverse = lax.rsqrt(jnp.mean(centred * centred, axis=1, keepdims=True) + EPSILON)
    normed = centred * inverse
    new_state = (state.astype(F32) + gain * normed * valid).astype(BF16)
    masked_up = upstream * valid
    gain_sum = jnp.sum(masked_up * normed, axis=0, keepdims=True)
    scaled = masked_up * gain
    grad_output = (
        inverse
        * (
            scaled
            - jnp.mean(scaled, axis=1, keepdims=True)
            - normed * jnp.mean(scaled * normed, axis=1, keepdims=True)
        )
    ).astype(BF16)
    grad_act = dot(grad_output, w_out_ref[...], (1, 1))
    slope = sigma * (1.0 + preact * (1.0 - sigma))
    grad_pre = (grad_act * slope).astype(BF16)
    return new_state, gain_sum, activated, grad_output, grad_pre


def inner_kernel(
    cfg,
    len_hbm,
    mask_hbm,
    state_hbm,
    tiles_hbm,
    up_hbm,
    w_in_hbm,
    w_out_hbm,
    gain_hbm,
    new_ref,
    own_ref,
    spread_ref,
    grad_in_ref,
    grad_out_ref,
    gain_sum_ref,
    rim_band_ref,
    rim_message_ref,
    rim_direct_ref,
    valid_ref,
    state_rim_ref,
    up_rim_ref,
    w_in_ref,
    w_out_ref,
    gain_ref,
    len_ref,
    mask_ref,
    state_ref,
    tiles_ref,
    up_ref,
    ext_ref,
    band_ref,
    sems,
):
    bs, offsets = cfg
    rim = (offsets - 1) // 2 * bs
    rows, latent = state_ref.shape
    per = rim // bs
    blocks = rows // bs
    width = 3 * rim
    low, inner, high = pl.ds(0, rim), pl.ds(rim, rows - 2 * rim), pl.ds(rows - rim, rim)
    late = pl.ds(rim, rim)

    pairs = [(len_hbm, len_ref), (mask_hbm, mask_ref), (state_hbm, state_ref)]
    pairs += [(tiles_hbm.at[o], tiles_ref.at[o]) for o in range(offsets)]
    first = len(pairs)
    pairs += [(w_in_hbm, w_in_ref), (w_out_hbm, w_out_ref), (gain_hbm, gain_ref)]
    pairs += [(up_hbm.at[inner, :], up_ref)]
    second = len(pairs)
    pairs += [(state_hbm.at[low, :], state_rim_ref.at[low, :]), (state_hbm.at[high, :], state_rim_ref.at[late, :])]
    pairs += [(up_hbm.at[low, :], up_rim_ref.at[low, :]), (up_hbm.at[high, :], up_rim_ref.at[late, :])]
    copies = [pltpu.make_async_copy(a, b, sems.at[i]) for i, (a, b) in enumerate(pairs)]
    for copy in copies:
        copy.start()
    for copy in copies[:first]:
        copy.wait()

    valid_ref[...] = validity(len_ref, 0, blocks, bs)
    ext_ref[...] = (state_ref[...].astype(F32) * valid_ref[...]).astype(BF16)
    message = []
    for chunk in range(1, rows // rim - 1):
        band = band_ref.at[chunk - 1]
        fill_band(band, tiles_ref, mask_ref, chunk * per, per, bs, offsets)
        message.append(dot(band[...], ext_ref[(chunk - 1) * rim : (chunk - 1) * rim + width, :], (1, 0)))
    inner = slice(rim, rows - rim)
    valid = valid_ref[inner, :]
    message = (jnp.concatenate(message, axis=0) * valid).astype(BF16)
    for copy in copies[first:second]:
        copy.wait()
    state = state_ref[inner, :]
    upstream = up_ref[...].astype(F32)
    direct_part = dot(state, w_in_ref[:latent, :], (1, 0))
    new_state, gain_sum, activated, grad_output, grad_pre = node_rows(
        state, message, direct_part, upstream, valid, w_in_ref, w_out_ref, gain_ref[...]
    )
    new_ref[...] = new_state
    gain_sum_ref[...] = gain_sum
    grad_out_ref[...] = dot(activated, grad_output, (0, 0))
    grad_in_ref[:latent, :] = dot(state, grad_pre, (0, 0))
    grad_in_ref[latent:, :] = dot(message, grad_pre, (0, 0))
    own_ref[...] = upstream + dot(grad_pre, w_in_ref[:latent, :], (1, 1))
    grad_message = dot(grad_pre, w_in_ref[latent:, :], (1, 1)).astype(BF16)
    grad_message = (grad_message.astype(F32) * valid).astype(BF16)
    spread_ref[...] = jnp.zeros_like(spread_ref)
    for chunk in range(1, rows // rim - 1):
        reach = slice((chunk - 1) * rim, (chunk - 1) * rim + width)
        spread_ref[reach, :] += dot(
            band_ref[chunk - 1], grad_message[(chunk - 1) * rim : chunk * rim, :], (0, 0)
        )

    for end in range(2):
        first = end * (blocks - per)
        band = rim_band_ref.at[end]
        fill_band(band, tiles_ref, mask_ref, first, per, bs, offsets)
        here = slice(end * rim, (end + 1) * rim)
        if end == 0:
            rim_message_ref[here, :] = dot(band[:, rim:], ext_ref[: 2 * rim, :], (1, 0))
        else:
            rim_message_ref[here, :] = dot(band[:, : 2 * rim], ext_ref[rows - 2 * rim :, :], (1, 0))
        rim_direct_ref[here, :] = dot(
            state_ref[first * bs : first * bs + rim, :], w_in_ref[:latent, :], (1, 0)
        )
    for copy in copies[second:]:
        copy.wait()


def rim_kernel(
    scale,
    valid_ref,
    state_ref,
    up_ref,
    w_in_ref,
    w_out_ref,
    gain_ref,
    band_ref,
    message_ref,
    direct_ref,
    inner_in_ref,
    inner_out_ref,
    inner_gain_ref,
    odd_ref,
    even_ref,
    send_ref,
    new_ref,
    pre_ref,
    grad_in_ref,
    grad_out_ref,
):
    rows = valid_ref.shape[0]
    rim, latent = odd_ref.shape
    side, me = place()
    odd = odd_ref[...]
    even = even_ref[...]
    low = jnp.where(side == 0, odd, even)
    high = jnp.where(side == 0, even, odd)
    valid = jnp.concatenate([valid_ref[:rim, :], valid_ref[rows - rim :, :]], axis=0)
    arrived = jnp.concatenate(
        [dot(band_ref[0, :, :rim], low, (1, 0)), dot(band_ref[1, :, 2 * rim :], high, (1, 0))], axis=0
    )
    message = ((message_ref[...] + arrived) * valid).astype(BF16)
    state = state_ref[...]
    upstream = up_ref[...].astype(F32)
    new_state, gain_sum, activated, grad_output, grad_pre = node_rows(
        state, message, direct_ref[...], upstream, valid, w_in_ref, w_out_ref, gain_ref[...]
    )
    new_ref[...] = new_state
    gain_sum = gain_sum + inner_gain_ref[...]
    grad_out_ref[...] = inner_out_ref[...] + dot(activated, grad_output, (0, 0))
    grad_in_ref[:latent, :] = inner_in_ref[:latent, :] + dot(state, grad_pre, (0, 0))
    grad_in_ref[latent:, :] = inner_in_ref[latent:, :] + dot(message, grad_pre, (0, 0))
    pre_ref[...] = grad_pre

    count = send_ref.shape[0] * send_ref.shape[1]
    n_in = grad_in_ref.shape[0] // count
    n_out = grad_out_ref.shape[0] // count
    top = lax.broadcasted_iota(jnp.int32, (GAIN_ROWS, latent), 0) == 0
    for piece in range(count):
        turn = lax.bitwise_xor(me, piece)
        half = lax.bitwise_and(turn, 1)
        slot = lax.shift_right_logical(turn, 1)
        send_ref[half, slot, :n_in, :] = (grad_in_ref[piece * n_in : (piece + 1) * n_in, :] * scale).astype(BF16)
        send_ref[half, slot, n_in : n_in + n_out, :] = (
            grad_out_ref[piece * n_out : (piece + 1) * n_out, :] * scale
        ).astype(BF16)
        if piece == 0:
            tail = jnp.where(top, gain_sum * scale, 0.0)
        else:
            tail = jnp.zeros((GAIN_ROWS, latent), F32)
        send_ref[half, slot, n_in + n_out :, :] = tail.astype(BF16)


def back_kernel(
    valid_ref,
    up_ref,
    w_in_ref,
    band_ref,
    pre_ref,
    new_inner_ref,
    new_rim_ref,
    own_inner_ref,
    spread_inner_ref,
    spill_odd_ref,
    spill_even_ref,
    own_ref,
    new_ref,
    out_ref,
    inner_ref,
    sems,
):
    rim, latent = spill_odd_ref.shape
    rows = valid_ref.shape[0]
    side, _ = place()
    inner = pl.ds(rim, rows - 2 * rim)
    news = [
        pltpu.make_async_copy(new_rim_ref.at[pl.ds(0, rim), :], new_ref.at[pl.ds(0, rim), :], sems.at[0]),
        pltpu.make_async_copy(new_inner_ref, new_ref.at[inner, :], sems.at[1]),
        pltpu.make_async_copy(
            new_rim_ref.at[pl.ds(rim, rim), :], new_ref.at[pl.ds(rows - rim, rim), :], sems.at[2]
        ),
    ]
    for copy in news:
        copy.start()
    valid = jnp.concatenate([valid_ref[:rim, :], valid_ref[rows - rim :, :]], axis=0)
    grad_pre = pre_ref[...]
    grad_message = dot(grad_pre, w_in_ref[latent:, :], (1, 1)).astype(BF16)
    grad_message = (grad_message.astype(F32) * valid).astype(BF16)
    left = dot(band_ref[0], grad_message[:rim, :], (0, 0))
    right = dot(band_ref[1], grad_message[rim:, :], (0, 0))
    low = left[:rim, :].astype(BF16)
    high = right[2 * rim :, :].astype(BF16)
    spill_odd_ref[...] = jnp.where(side == 0, low, high)
    spill_even_ref[...] = jnp.where(side == 0, high, low)
    spread = spread_inner_ref[...] + jnp.concatenate([left[rim:, :], right[: 2 * rim, :]], axis=0)
    spread = spread * valid_ref[...]
    inner_ref[...] = (own_inner_ref[...] + spread[rim : rows - rim, :]).astype(BF16)
    inside = pltpu.make_async_copy(inner_ref, out_ref.at[inner, :], sems.at[3])
    inside.start()
    own = up_ref[...].astype(F32) + dot(grad_pre, w_in_ref[:latent, :], (1, 1))
    own_ref[...] = own + jnp.concatenate([spread[:rim, :], spread[rows - rim :, :]], axis=0)
    for copy in news:
        copy.wait()
    inside.wait()


def finish_kernel(started_ref, valid_ref, own_ref, odd_ref, even_ref, out_ref, held_ref, sems):
    rows = valid_ref.shape[0]
    rim = odd_ref.shape[0]
    side, _ = place()
    odd = odd_ref[...].astype(F32)
    even = even_ref[...].astype(F32)
    copies = []
    for end in range(2):
        first = end * (rows - rim)
        there = slice(end * rim, (end + 1) * rim)
        back = jnp.where(side == end, odd, even)
        held_ref[there, :] = (own_ref[there, :] + back * valid_ref[first : first + rim, :]).astype(BF16)
        copy = pltpu.make_async_copy(
            held_ref.at[pl.ds(end * rim, rim), :], out_ref.at[pl.ds(first, rim), :], sems.at[end]
        )
        copy.start()
        copies.append(copy)
    for copy in copies:
        copy.wait()


def unpack_kernel(*refs):
    pieces = refs[:-3]
    grad_in_ref, grad_out_ref, gain_ref = refs[-3:]
    _, me = place()
    count = len(pieces)
    n_in = grad_in_ref.shape[0] // count
    n_out = grad_out_ref.shape[0] // count
    for turn in range(count):
        source = pieces[turn // 2 + turn % 2 * (count // 2)]
        piece = lax.bitwise_xor(me, turn)
        at_in = pl.ds(pl.multiple_of(piece * n_in, n_in), n_in)
        at_out = pl.ds(pl.multiple_of(piece * n_out, n_out), n_out)
        grad_in_ref[at_in, :] = source[:n_in, :].astype(F32)
        grad_out_ref[at_out, :] = source[n_in : n_in + n_out, :].astype(F32)

        @pl.when(piece == 0)
        def _():
            gain_ref[...] = source[n_in + n_out :, :].astype(F32)[:1, :]


def swap(x, axis, turn):
    count = lax.axis_size(axis)
    return lax.ppermute(x, axis, [(i, i ^ turn) for i in range(count)])


def gathered(x, axis):
    count = lax.axis_size(axis)
    if count & (count - 1) == 0:
        return [x] + [swap(x, axis, k) for k in range(1, count)]
    moved = [x] + [
        lax.ppermute(x, axis, [(i, (i + k) % count) for i in range(count)]) for k in range(1, count)
    ]
    order = (lax.axis_index(axis) - jnp.arange(count)) % count
    stacked = jnp.stack(moved)[order]
    return [stacked[k] for k in range(count)]


def tree_sum(parts):
    parts = [part.astype(F32) for part in parts]
    while len(parts) > 1:
        paired = [parts[i] + parts[i + 1] for i in range(0, len(parts) - 1, 2)]
        parts = paired + parts[len(parts) - len(parts) % 2 :]
    return parts[0]


def vmem(count):
    return [pl.BlockSpec(memory_space=pltpu.VMEM)] * count


def shapes(*given):
    return tuple(jax.ShapeDtypeStruct(shape, dtype) for shape, dtype in given)


def kernel(body, name, inputs, outputs, scratch=(), flops=0, moved=0, aliases=None):
    far, arrays = inputs
    spaces = [out.memory_space if hasattr(out, "memory_space") else pltpu.VMEM for out in outputs]
    call = pl.pallas_call(
        body,
        out_shape=outputs,
        in_specs=[pl.BlockSpec(memory_space=pltpu.HBM)] * far + vmem(arrays),
        out_specs=tuple(pl.BlockSpec(memory_space=space) for space in spaces),
        scratch_shapes=list(scratch),
        input_output_aliases=aliases or {},
        compiler_params=pltpu.CompilerParams(vmem_limit_bytes=VMEM_LIMIT),
        cost_estimate=pl.CostEstimate(flops=flops, bytes_accessed=moved, transcendentals=0),
        name=name,
    )

    def run(*given):
        placed = [pltpu.with_memory_space_constraint(x, pltpu.HBM) for x in given[:far]]
        return call(*placed, *given[far:])

    return run


def local(node_state, edge_tiles, block_mask, block_len, w_in, w_out, gain, upstream):
    rows, latent = node_state.shape
    offsets, bs = edge_tiles.shape[1:]
    rim = (offsets - 1) // 2 * bs
    inside = rows - 2 * rim
    width = 3 * rim
    dom = lax.axis_size("dom")
    rep = lax.axis_size("rep")
    total = dom * rep
    scale = 1.0 / math.sqrt(rows * total)
    ring = ("dom", "rep")
    even_pairs = [(i, i ^ 1) for i in range(total)]
    odd_pairs = [(i, (i + 1) % total if i % 2 else (i - 1) % total) for i in range(total)]
    gain_row = gain.reshape(1, latent)
    tiles = jnp.transpose(edge_tiles, (1, 0, 2))

    to_odd, to_even = kernel(
        functools.partial(pack_kernel, bs),
        "pack_rims",
        (2, 0),
        shapes(((rim, latent), BF16), ((rim, latent), BF16)),
        [
            pltpu.VMEM((2, rim, latent), BF16),
            pltpu.SMEM(block_len.shape, jnp.int32),
            pltpu.SemaphoreType.DMA((3,)),
        ],
    )(block_len, node_state)
    from_odd = lax.ppermute(to_odd, ring, odd_pairs)
    from_even = lax.ppermute(to_even, ring, even_pairs)

    work = 2 * inside * latent * (width + 5 * latent + 2 * latent + 2 * latent + width)
    new_inner, own_inner, spread_inner, sum_in, sum_out, sum_gain, band, message, direct, *kept = kernel(
        functools.partial(inner_kernel, (bs, offsets)),
        "inner_rows",
        (8, 0),
        shapes(
            ((inside, latent), BF16),
            ((inside, latent), F32),
            ((rows, latent), F32),
            (w_in.shape, F32),
            (w_out.shape, F32),
            ((1, latent), F32),
            ((2, rim, width), BF16),
            ((2 * rim, latent), F32),
            ((2 * rim, latent), F32),
            ((rows, 1), F32),
            ((2 * rim, latent), BF16),
            ((2 * rim, latent), BF16),
            (w_in.shape, BF16),
            (w_out.shape, BF16),
            ((1, latent), F32),
        ),
        [
            pltpu.SMEM(block_len.shape, jnp.int32),
            pltpu.SMEM(block_mask.shape, jnp.int32),
            pltpu.VMEM((rows, latent), BF16),
            pltpu.VMEM(tiles.shape, BF16),
            pltpu.VMEM((inside, latent), BF16),
            pltpu.VMEM((rows, latent), BF16),
            pltpu.VMEM((inside // rim, rim, width), BF16),
            pltpu.SemaphoreType.DMA((11 + offsets,)),
        ],
        flops=work,
        moved=10 * 1024 * 1024,
    )(block_len, block_mask, node_state, tiles, upstream, w_in, w_out, gain_row)

    n_in, n_out = w_in.shape[0] // dom, w_out.shape[0] // dom
    piece_rows = n_in + n_out + GAIN_ROWS
    send, new_rim, pre_rim = kernel(
        functools.partial(rim_kernel, scale),
        "rim_rows",
        (0, 14),
        shapes(
            ((2, dom // 2, piece_rows, latent), BF16),
            ((2 * rim, latent), BF16),
            ((2 * rim, latent), BF16),
        ),
        [pltpu.VMEM(w_in.shape, F32), pltpu.VMEM(w_out.shape, F32)],
        flops=work,
        moved=8 * 1024 * 1024,
    )(
        *kept,
        band, message, direct, sum_in, sum_out, sum_gain, from_odd, from_even,
    )

    valid, _, up_rim, w_in_near, _, _ = kept
    other = swap(send[1], "dom", 1)
    held = (send[0].astype(F32) + other.astype(F32)).astype(BF16)
    held = [held[k] for k in range(dom // 2)]
    spill_odd, spill_even, own_rim, new_state, grad_state = kernel(
        back_kernel,
        "rim_back",
        (0, 9),
        shapes(((rim, latent), BF16), ((rim, latent), BF16), ((2 * rim, latent), F32))
        + (pltpu.HBM((rows, latent), BF16), pltpu.HBM((rows, latent), BF16)),
        [pltpu.VMEM((inside, latent), BF16), pltpu.SemaphoreType.DMA((4,))],
        flops=2 * inside * latent * (2 * latent + width),
        moved=4 * 1024 * 1024,
    )(valid, up_rim, w_in_near, band, pre_rim, new_inner, new_rim, own_inner, spread_inner)

    parts = [held[0]] + [swap(held[k], "dom", 2 * k) for k in range(1, dom // 2)]
    quarter = sum(part.astype(F32) for part in parts).astype(BF16)
    planes = gathered(quarter, "rep")
    back_odd = lax.ppermute(spill_odd, ring, odd_pairs)
    back_even = lax.ppermute(spill_even, ring, even_pairs)
    mine = tree_sum(planes).astype(BF16)
    near = [mine] + [swap(mine, "dom", 2 * k) for k in range(1, dom // 2)]
    near[-1], back_odd, back_even = lax.optimization_barrier((near[-1], back_odd, back_even))
    (grad_state,) = kernel(
        finish_kernel,
        "finish_state",
        (1, 4),
        (pltpu.HBM((rows, latent), BF16),),
        [pltpu.VMEM((2 * rim, latent), BF16), pltpu.SemaphoreType.DMA((2,))],
        aliases={0: 0},
    )(grad_state, valid, own_rim, back_odd, back_even)
    other = swap(jnp.stack(near), "dom", 1)
    other = [other[k] for k in range(dom // 2)]
    *other, grad_state = lax.optimization_barrier((*other, grad_state))
    grad_w_in, grad_w_out, grad_gain = kernel(
        unpack_kernel,
        "unpack_sums",
        (0, dom),
        shapes((w_in.shape, F32), (w_out.shape, F32), ((1, latent), F32)),
    )(*near, *other)
    return new_state, grad_state, grad_w_in, grad_w_out, grad_gain.reshape(latent)


def solution(mesh):
    placed = (
        P(("dom", "rep"), None),
        P(("dom", "rep"), None, None),
        P(("dom", "rep"), None),
        P(("dom", "rep")),
        P(),
        P(),
        P(),
        P(("dom", "rep"), None),
    )
    return jax.shard_map(
        local,
        mesh=mesh,
        in_specs=placed,
        out_specs=(P(("dom", "rep"), None), P(("dom", "rep"), None), P(), P(), P()),
        check_vma=False,
    )
```

```python
import functools
import math

import jax
import jax.numpy as jnp
from jax import lax
from jax.experimental import pallas as pl
from jax.experimental.pallas import tpu as pltpu
from jax.sharding import PartitionSpec as P

EPSILON = 1e-05
F32 = jnp.float32
BF16 = jnp.bfloat16
GAIN_ROWS = 8
VMEM_LIMIT = 40 * 1024 * 1024


def dot(a, b, contract):
    return lax.dot_general(a, b, ((contract[:1], contract[1:]), ((), ())), preferred_element_type=F32)


def sublane(bs):
    return lax.broadcasted_iota(jnp.int32, (bs, 1), 0)


def validity(len_ref, first, count, bs):
    return jnp.concatenate(
        [(sublane(bs) < len_ref[first + j]).astype(F32) for j in range(count)], axis=0
    )


def place():
    me = lax.axis_index("dom")
    index = me * lax.axis_size("rep") + lax.axis_index("rep")
    return lax.rem(index, 2), me


def pack_kernel(bs, len_ref, state_ref, first_ref, last_ref, held_ref, lens_ref, sems):
    rows = state_ref.shape[0]
    rim = first_ref.shape[0]
    per = rim // bs
    copies = [
        pltpu.make_async_copy(len_ref, lens_ref, sems.at[0]),
        pltpu.make_async_copy(state_ref.at[pl.ds(rows - rim, rim), :], held_ref.at[1], sems.at[1]),
        pltpu.make_async_copy(state_ref.at[pl.ds(0, rim), :], held_ref.at[0], sems.at[2]),
    ]
    for copy in copies:
        copy.start()
    for copy in copies:
        copy.wait()
    blocks = rows // bs
    for j in range(per):
        here = slice(j * bs, (j + 1) * bs)
        first_ref[here, :] = held_ref[0, here, :] * (sublane(bs) < lens_ref[j]).astype(F32).astype(BF16)
        last_ref[here, :] = held_ref[1, here, :] * (
            sublane(bs) < lens_ref[blocks - per + j]
        ).astype(F32).astype(BF16)


def fill_band(band_ref, tiles_ref, mask_ref, first, per, bs, offsets):
    for j in range(per):
        row = slice(j * bs, (j + 1) * bs)
        for column in range(per + offsets - 1):
            offset = column - j
            cols = slice(column * bs, (column + 1) * bs)
            if 0 <= offset < offsets:
                tile = tiles_ref[offset, (first + j) * bs : (first + j + 1) * bs, :]
                band_ref[row, cols] = tile * mask_ref[first + j, offset].astype(F32).astype(BF16)
            else:
                band_ref[row, cols] = jnp.zeros((bs, bs), BF16)


def node_rows(state, message, direct_part, upstream, valid, w_in_ref, w_out_ref, gain):
    latent = state.shape[1]
    preact = direct_part + dot(message, w_in_ref[latent:, :], (1, 0))
    sigma = jax.nn.sigmoid(preact)
    activated = (preact * sigma).astype(BF16)
    output = dot(activated, w_out_ref[...], (1, 0))
    centred = output - jnp.mean(output, axis=1, keepdims=True)
    inverse = lax.rsqrt(jnp.mean(centred * centred, axis=1, keepdims=True) + EPSILON)
    normed = centred * inverse
    new_state = (state.astype(F32) + gain * normed * valid).astype(BF16)
    masked_up = upstream * valid
    gain_sum = jnp.sum(masked_up * normed, axis=0, keepdims=True)
    scaled = masked_up * gain
    grad_output = (
        inverse
        * (
            scaled
            - jnp.mean(scaled, axis=1, keepdims=True)
            - normed * jnp.mean(scaled * normed, axis=1, keepdims=True)
        )
    ).astype(BF16)
    grad_act = dot(grad_output, w_out_ref[...], (1, 1))
    slope = sigma * (1.0 + preact * (1.0 - sigma))
    grad_pre = (grad_act * slope).astype(BF16)
    return new_state, gain_sum, activated, grad_output, grad_pre


def inner_kernel(
    cfg,
    len_hbm,
    mask_hbm,
    state_hbm,
    tiles_hbm,
    up_hbm,
    w_in_hbm,
    w_out_hbm,
    gain_hbm,
    new_ref,
    own_ref,
    spread_ref,
    grad_in_ref,
    grad_out_ref,
    gain_sum_ref,
    rim_band_ref,
    rim_message_ref,
    rim_direct_ref,
    valid_ref,
    state_rim_ref,
    up_rim_ref,
    w_in_ref,
    w_out_ref,
    gain_ref,
    len_ref,
    mask_ref,
    state_ref,
    tiles_ref,
    up_ref,
    ext_ref,
    band_ref,
    sems,
):
    bs, offsets = cfg
    rim = (offsets - 1) // 2 * bs
    rows, latent = state_ref.shape
    per = rim // bs
    blocks = rows // bs
    width = 3 * rim
    low, inner, high = pl.ds(0, rim), pl.ds(rim, rows - 2 * rim), pl.ds(rows - rim, rim)
    late = pl.ds(rim, rim)

    pairs = [(len_hbm, len_ref), (mask_hbm, mask_ref), (state_hbm, state_ref)]
    pairs += [(tiles_hbm.at[o], tiles_ref.at[o]) for o in range(offsets)]
    first = len(pairs)
    pairs += [(w_in_hbm, w_in_ref), (w_out_hbm, w_out_ref), (gain_hbm, gain_ref)]
    pairs += [(up_hbm.at[inner, :], up_ref)]
    second = len(pairs)
    pairs += [(state_hbm.at[low, :], state_rim_ref.at[low, :]), (state_hbm.at[high, :], state_rim_ref.at[late, :])]
    pairs += [(up_hbm.at[low, :], up_rim_ref.at[low, :]), (up_hbm.at[high, :], up_rim_ref.at[late, :])]
    copies = [pltpu.make_async_copy(a, b, sems.at[i]) for i, (a, b) in enumerate(pairs)]
    for copy in copies:
        copy.start()
    for copy in copies[:first]:
        copy.wait()

    valid_ref[...] = validity(len_ref, 0, blocks, bs)
    ext_ref[...] = (state_ref[...].astype(F32) * valid_ref[...]).astype(BF16)
    message = []
    for chunk in range(1, rows // rim - 1):
        band = band_ref.at[chunk - 1]
        fill_band(band, tiles_ref, mask_ref, chunk * per, per, bs, offsets)
        message.append(dot(band[...], ext_ref[(chunk - 1) * rim : (chunk - 1) * rim + width, :], (1, 0)))
    inner = slice(rim, rows - rim)
    valid = valid_ref[inner, :]
    message = (jnp.concatenate(message, axis=0) * valid).astype(BF16)
    for copy in copies[first:second]:
        copy.wait()
    state = state_ref[inner, :]
    upstream = up_ref[...].astype(F32)
    direct_part = dot(state, w_in_ref[:latent, :], (1, 0))
    new_state, gain_sum, activated, grad_output, grad_pre = node_rows(
        state, message, direct_part, upstream, valid, w_in_ref, w_out_ref, gain_ref[...]
    )
    new_ref[...] = new_state
    gain_sum_ref[...] = gain_sum
    grad_out_ref[...] = dot(activated, grad_output, (0, 0))
    grad_in_ref[:latent, :] = dot(state, grad_pre, (0, 0))
    grad_in_ref[latent:, :] = dot(message, grad_pre, (0, 0))
    own_ref[...] = upstream + dot(grad_pre, w_in_ref[:latent, :], (1, 1))
    grad_message = dot(grad_pre, w_in_ref[latent:, :], (1, 1)).astype(BF16)
    grad_message = (grad_message.astype(F32) * valid).astype(BF16)
    spread_ref[...] = jnp.zeros_like(spread_ref)
    for chunk in range(1, rows // rim - 1):
        reach = slice((chunk - 1) * rim, (chunk - 1) * rim + width)
        spread_ref[reach, :] += dot(
            band_ref[chunk - 1], grad_message[(chunk - 1) * rim : chunk * rim, :], (0, 0)
        )

    for end in range(2):
        first = end * (blocks - per)
        band = rim_band_ref.at[end]
        fill_band(band, tiles_ref, mask_ref, first, per, bs, offsets)
        here = slice(end * rim, (end + 1) * rim)
        if end == 0:
            rim_message_ref[here, :] = dot(band[:, rim:], ext_ref[: 2 * rim, :], (1, 0))
        else:
            rim_message_ref[here, :] = dot(band[:, : 2 * rim], ext_ref[rows - 2 * rim :, :], (1, 0))
        rim_direct_ref[here, :] = dot(
            state_ref[first * bs : first * bs + rim, :], w_in_ref[:latent, :], (1, 0)
        )
    for copy in copies[second:]:
        copy.wait()


def rim_kernel(
    scale,
    valid_ref,
    state_ref,
    up_ref,
    w_in_ref,
    w_out_ref,
    gain_ref,
    band_ref,
    message_ref,
    direct_ref,
    inner_in_ref,
    inner_out_ref,
    inner_gain_ref,
    low_ref,
    high_ref,
    send_ref,
    new_ref,
    pre_ref,
    grad_in_ref,
    grad_out_ref,
):
    rows = valid_ref.shape[0]
    rim, latent = low_ref.shape
    _, me = place()
    valid = jnp.concatenate([valid_ref[:rim, :], valid_ref[rows - rim :, :]], axis=0)
    arrived = jnp.concatenate(
        [dot(band_ref[0, :, :rim], low_ref[...], (1, 0)), dot(band_ref[1, :, 2 * rim :], high_ref[...], (1, 0))], axis=0
    )
    message = ((message_ref[...] + arrived) * valid).astype(BF16)
    state = state_ref[...]
    upstream = up_ref[...].astype(F32)
    new_state, gain_sum, activated, grad_output, grad_pre = node_rows(
        state, message, direct_ref[...], upstream, valid, w_in_ref, w_out_ref, gain_ref[...]
    )
    new_ref[...] = new_state
    gain_sum = gain_sum + inner_gain_ref[...]
    grad_out_ref[...] = inner_out_ref[...] + dot(activated, grad_output, (0, 0))
    grad_in_ref[:latent, :] = inner_in_ref[:latent, :] + dot(state, grad_pre, (0, 0))
    grad_in_ref[latent:, :] = inner_in_ref[latent:, :] + dot(message, grad_pre, (0, 0))
    pre_ref[...] = grad_pre

    count = send_ref.shape[0] * send_ref.shape[1]
    n_in = grad_in_ref.shape[0] // count
    n_out = grad_out_ref.shape[0] // count
    top = lax.broadcasted_iota(jnp.int32, (GAIN_ROWS, latent), 0) == 0
    for piece in range(count):
        turn = lax.bitwise_xor(me, piece)
        half = lax.bitwise_and(turn, 1)
        slot = lax.shift_right_logical(turn, 1)
        send_ref[half, slot, :n_in, :] = (grad_in_ref[piece * n_in : (piece + 1) * n_in, :] * scale).astype(BF16)
        send_ref[half, slot, n_in : n_in + n_out, :] = (
            grad_out_ref[piece * n_out : (piece + 1) * n_out, :] * scale
        ).astype(BF16)
        if piece == 0:
            tail = jnp.where(top, gain_sum * scale, 0.0)
        else:
            tail = jnp.zeros((GAIN_ROWS, latent), F32)
        send_ref[half, slot, n_in + n_out :, :] = tail.astype(BF16)


def back_kernel(
    valid_ref,
    up_ref,
    w_in_ref,
    band_ref,
    pre_ref,
    new_inner_ref,
    new_rim_ref,
    own_inner_ref,
    spread_inner_ref,
    spill_odd_ref,
    spill_even_ref,
    own_ref,
    new_ref,
    out_ref,
    inner_ref,
    sems,
):
    rim, latent = spill_odd_ref.shape
    rows = valid_ref.shape[0]
    side, _ = place()
    inner = pl.ds(rim, rows - 2 * rim)
    news = [
        pltpu.make_async_copy(new_rim_ref.at[pl.ds(0, rim), :], new_ref.at[pl.ds(0, rim), :], sems.at[0]),
        pltpu.make_async_copy(new_inner_ref, new_ref.at[inner, :], sems.at[1]),
        pltpu.make_async_copy(
            new_rim_ref.at[pl.ds(rim, rim), :], new_ref.at[pl.ds(rows - rim, rim), :], sems.at[2]
        ),
    ]
    for copy in news:
        copy.start()
    valid = jnp.concatenate([valid_ref[:rim, :], valid_ref[rows - rim :, :]], axis=0)
    grad_pre = pre_ref[...]
    grad_message = dot(grad_pre, w_in_ref[latent:, :], (1, 1)).astype(BF16)
    grad_message = (grad_message.astype(F32) * valid).astype(BF16)
    left = dot(band_ref[0], grad_message[:rim, :], (0, 0))
    right = dot(band_ref[1], grad_message[rim:, :], (0, 0))
    low = left[:rim, :].astype(BF16)
    high = right[2 * rim :, :].astype(BF16)
    spill_odd_ref[...] = jnp.where(side == 0, low, high)
    spill_even_ref[...] = jnp.where(side == 0, high, low)
    spread = spread_inner_ref[...] + jnp.concatenate([left[rim:, :], right[: 2 * rim, :]], axis=0)
    spread = spread * valid_ref[...]
    inner_ref[...] = (own_inner_ref[...] + spread[rim : rows - rim, :]).astype(BF16)
    inside = pltpu.make_async_copy(inner_ref, out_ref.at[inner, :], sems.at[3])
    inside.start()
    own = up_ref[...].astype(F32) + dot(grad_pre, w_in_ref[:latent, :], (1, 1))
    own_ref[...] = own + jnp.concatenate([spread[:rim, :], spread[rows - rim :, :]], axis=0)
    for copy in news:
        copy.wait()
    inside.wait()


def finish_kernel(started_ref, valid_ref, own_ref, odd_ref, even_ref, out_ref, held_ref, sems):
    rows = valid_ref.shape[0]
    rim = odd_ref.shape[0]
    side, _ = place()
    odd = odd_ref[...].astype(F32)
    even = even_ref[...].astype(F32)
    copies = []
    for end in range(2):
        first = end * (rows - rim)
        there = slice(end * rim, (end + 1) * rim)
        back = jnp.where(side == end, odd, even)
        held_ref[there, :] = (own_ref[there, :] + back * valid_ref[first : first + rim, :]).astype(BF16)
        copy = pltpu.make_async_copy(
            held_ref.at[pl.ds(end * rim, rim), :], out_ref.at[pl.ds(first, rim), :], sems.at[end]
        )
        copy.start()
        copies.append(copy)
    for copy in copies:
        copy.wait()


def unpack_kernel(*refs):
    pieces = refs[:-3]
    grad_in_ref, grad_out_ref, gain_ref = refs[-3:]
    _, me = place()
    count = len(pieces)
    n_in = grad_in_ref.shape[0] // count
    n_out = grad_out_ref.shape[0] // count
    for turn in range(count):
        source = pieces[turn // 2 + turn % 2 * (count // 2)]
        piece = lax.bitwise_xor(me, turn)
        at_in = pl.ds(pl.multiple_of(piece * n_in, n_in), n_in)
        at_out = pl.ds(pl.multiple_of(piece * n_out, n_out), n_out)
        grad_in_ref[at_in, :] = source[:n_in, :].astype(F32)
        grad_out_ref[at_out, :] = source[n_in : n_in + n_out, :].astype(F32)

        @pl.when(piece == 0)
        def _():
            gain_ref[...] = source[n_in + n_out :, :].astype(F32)[:1, :]


def swap(x, axis, turn):
    count = lax.axis_size(axis)
    return lax.ppermute(x, axis, [(i, i ^ turn) for i in range(count)])


def gathered(x, axis):
    count = lax.axis_size(axis)
    if count & (count - 1) == 0:
        return [x] + [swap(x, axis, k) for k in range(1, count)]
    moved = [x] + [
        lax.ppermute(x, axis, [(i, (i + k) % count) for i in range(count)]) for k in range(1, count)
    ]
    order = (lax.axis_index(axis) - jnp.arange(count)) % count
    stacked = jnp.stack(moved)[order]
    return [stacked[k] for k in range(count)]


def tree_sum(parts):
    parts = [part.astype(F32) for part in parts]
    while len(parts) > 1:
        paired = [parts[i] + parts[i + 1] for i in range(0, len(parts) - 1, 2)]
        parts = paired + parts[len(parts) - len(parts) % 2 :]
    return parts[0]


def vmem(count):
    return [pl.BlockSpec(memory_space=pltpu.VMEM)] * count


def shapes(*given):
    return tuple(jax.ShapeDtypeStruct(shape, dtype) for shape, dtype in given)


def kernel(body, name, inputs, outputs, scratch=(), flops=0, moved=0, aliases=None):
    far, arrays = inputs
    spaces = [out.memory_space if hasattr(out, "memory_space") else pltpu.VMEM for out in outputs]
    call = pl.pallas_call(
        body,
        out_shape=outputs,
        in_specs=[pl.BlockSpec(memory_space=pltpu.HBM)] * far + vmem(arrays),
        out_specs=tuple(pl.BlockSpec(memory_space=space) for space in spaces),
        scratch_shapes=list(scratch),
        input_output_aliases=aliases or {},
        compiler_params=pltpu.CompilerParams(vmem_limit_bytes=VMEM_LIMIT),
        cost_estimate=pl.CostEstimate(flops=flops, bytes_accessed=moved, transcendentals=0),
        name=name,
    )

    def run(*given):
        placed = [pltpu.with_memory_space_constraint(x, pltpu.HBM) for x in given[:far]]
        return call(*placed, *given[far:])

    return run


def local(node_state, edge_tiles, block_mask, block_len, w_in, w_out, gain, upstream):
    rows, latent = node_state.shape
    offsets, bs = edge_tiles.shape[1:]
    rim = (offsets - 1) // 2 * bs
    inside = rows - 2 * rim
    width = 3 * rim
    dom = lax.axis_size("dom")
    rep = lax.axis_size("rep")
    total = dom * rep
    scale = 1.0 / math.sqrt(rows * total)
    ring = ("dom", "rep")
    next_pairs = [(i, (i + 1) % total) for i in range(total)]
    back_pairs = [(i, (i - 1) % total) for i in range(total)]
    even_pairs = [(i, i ^ 1) for i in range(total)]
    odd_pairs = [(i, (i + 1) % total if i % 2 else (i - 1) % total) for i in range(total)]
    gain_row = gain.reshape(1, latent)
    tiles = jnp.transpose(edge_tiles, (1, 0, 2))

    to_back, to_next = kernel(
        functools.partial(pack_kernel, bs),
        "pack_rims",
        (2, 0),
        shapes(((rim, latent), BF16), ((rim, latent), BF16)),
        [
            pltpu.VMEM((2, rim, latent), BF16),
            pltpu.SMEM(block_len.shape, jnp.int32),
            pltpu.SemaphoreType.DMA((3,)),
        ],
    )(block_len, node_state)
    from_back = lax.ppermute(to_next, ring, next_pairs)
    from_next = lax.ppermute(to_back, ring, back_pairs)

    work = 2 * inside * latent * (width + 5 * latent + 2 * latent + 2 * latent + width)
    new_inner, own_inner, spread_inner, sum_in, sum_out, sum_gain, band, message, direct, *kept = kernel(
        functools.partial(inner_kernel, (bs, offsets)),
        "inner_rows",
        (8, 0),
        shapes(
            ((inside, latent), BF16),
            ((inside, latent), F32),
            ((rows, latent), F32),
            (w_in.shape, F32),
            (w_out.shape, F32),
            ((1, latent), F32),
            ((2, rim, width), BF16),
            ((2 * rim, latent), F32),
            ((2 * rim, latent), F32),
            ((rows, 1), F32),
            ((2 * rim, latent), BF16),
            ((2 * rim, latent), BF16),
            (w_in.shape, BF16),
            (w_out.shape, BF16),
            ((1, latent), F32),
        ),
        [
            pltpu.SMEM(block_len.shape, jnp.int32),
            pltpu.SMEM(block_mask.shape, jnp.int32),
            pltpu.VMEM((rows, latent), BF16),
            pltpu.VMEM(tiles.shape, BF16),
            pltpu.VMEM((inside, latent), BF16),
            pltpu.VMEM((rows, latent), BF16),
            pltpu.VMEM((inside // rim, rim, width), BF16),
            pltpu.SemaphoreType.DMA((11 + offsets,)),
        ],
        flops=work,
        moved=10 * 1024 * 1024,
    )(block_len, block_mask, node_state, tiles, upstream, w_in, w_out, gain_row)

    n_in, n_out = w_in.shape[0] // dom, w_out.shape[0] // dom
    piece_rows = n_in + n_out + GAIN_ROWS
    send, new_rim, pre_rim = kernel(
        functools.partial(rim_kernel, scale),
        "rim_rows",
        (0, 14),
        shapes(
            ((2, dom // 2, piece_rows, latent), BF16),
            ((2 * rim, latent), BF16),
            ((2 * rim, latent), BF16),
        ),
        [pltpu.VMEM(w_in.shape, F32), pltpu.VMEM(w_out.shape, F32)],
        flops=work,
        moved=8 * 1024 * 1024,
    )(
        *kept,
        band, message, direct, sum_in, sum_out, sum_gain, from_back, from_next,
    )

    valid, _, up_rim, w_in_near, _, _ = kept
    other = swap(send[1], "dom", 1)
    held = (send[0].astype(F32) + other.astype(F32)).astype(BF16)
    held = [held[k] for k in range(dom // 2)]
    spill_odd, spill_even, own_rim, new_state, grad_state = kernel(
        back_kernel,
        "rim_back",
        (0, 9),
        shapes(((rim, latent), BF16), ((rim, latent), BF16), ((2 * rim, latent), F32))
        + (pltpu.HBM((rows, latent), BF16), pltpu.HBM((rows, latent), BF16)),
        [pltpu.VMEM((inside, latent), BF16), pltpu.SemaphoreType.DMA((4,))],
        flops=2 * inside * latent * (2 * latent + width),
        moved=4 * 1024 * 1024,
    )(valid, up_rim, w_in_near, band, pre_rim, new_inner, new_rim, own_inner, spread_inner)

    parts = [held[0]] + [swap(held[k], "dom", 2 * k) for k in range(1, dom // 2)]
    quarter = sum(part.astype(F32) for part in parts).astype(BF16)
    planes = gathered(quarter, "rep")
    back_odd = lax.ppermute(spill_odd, ring, odd_pairs)
    back_even = lax.ppermute(spill_even, ring, even_pairs)
    mine = tree_sum(planes).astype(BF16)
    near = [mine] + [swap(mine, "dom", 2 * k) for k in range(1, dom // 2)]
    near[-1], back_odd, back_even = lax.optimization_barrier((near[-1], back_odd, back_even))
    (grad_state,) = kernel(
        finish_kernel,
        "finish_state",
        (1, 4),
        (pltpu.HBM((rows, latent), BF16),),
        [pltpu.VMEM((2 * rim, latent), BF16), pltpu.SemaphoreType.DMA((2,))],
        aliases={0: 0},
    )(grad_state, valid, own_rim, back_odd, back_even)
    other = swap(jnp.stack(near), "dom", 1)
    other = [other[k] for k in range(dom // 2)]
    *other, grad_state = lax.optimization_barrier((*other, grad_state))
    grad_w_in, grad_w_out, grad_gain = kernel(
        unpack_kernel,
        "unpack_sums",
        (0, dom),
        shapes((w_in.shape, F32), (w_out.shape, F32), ((1, latent), F32)),
    )(*near, *other)
    return new_state, grad_state, grad_w_in, grad_w_out, grad_gain.reshape(latent)


def solution(mesh):
    placed = (
        P(("dom", "rep"), None),
        P(("dom", "rep"), None, None),
        P(("dom", "rep"), None),
        P(("dom", "rep")),
        P(),
        P(),
        P(),
        P(("dom", "rep"), None),
    )
    return jax.shard_map(
        local,
        mesh=mesh,
        in_specs=placed,
        out_specs=(P(("dom", "rep"), None), P(("dom", "rep"), None), P(), P(), P()),
        check_vma=False,
    )
```

```python
import functools
import math

import jax
import jax.numpy as jnp
from jax import lax
from jax.experimental import pallas as pl
from jax.experimental.pallas import tpu as pltpu
from jax.sharding import PartitionSpec as P

EPSILON = 1e-05
F32 = jnp.float32
BF16 = jnp.bfloat16
GAIN_ROWS = 8
VMEM_LIMIT = 40 * 1024 * 1024


def dot(a, b, contract):
    return lax.dot_general(a, b, ((contract[:1], contract[1:]), ((), ())), preferred_element_type=F32)


def sublane(bs):
    return lax.broadcasted_iota(jnp.int32, (bs, 1), 0)


def validity(len_ref, first, count, bs):
    return jnp.concatenate(
        [(sublane(bs) < len_ref[first + j]).astype(F32) for j in range(count)], axis=0
    )


def place():
    me = lax.axis_index("dom")
    index = me * lax.axis_size("rep") + lax.axis_index("rep")
    return lax.rem(index, 2), me


def pack_kernel(bs, len_ref, state_ref, first_ref, last_ref, held_ref, lens_ref, sems):
    rows = state_ref.shape[0]
    rim = first_ref.shape[0]
    per = rim // bs
    copies = [
        pltpu.make_async_copy(len_ref, lens_ref, sems.at[0]),
        pltpu.make_async_copy(state_ref.at[pl.ds(rows - rim, rim), :], held_ref.at[1], sems.at[1]),
        pltpu.make_async_copy(state_ref.at[pl.ds(0, rim), :], held_ref.at[0], sems.at[2]),
    ]
    for copy in copies:
        copy.start()
    for copy in copies:
        copy.wait()
    blocks = rows // bs
    for j in range(per):
        here = slice(j * bs, (j + 1) * bs)
        first_ref[here, :] = held_ref[0, here, :] * (sublane(bs) < lens_ref[j]).astype(F32).astype(BF16)
        last_ref[here, :] = held_ref[1, here, :] * (
            sublane(bs) < lens_ref[blocks - per + j]
        ).astype(F32).astype(BF16)


def fill_band(band_ref, tiles_ref, mask_ref, first, per, bs, offsets):
    for j in range(per):
        row = slice(j * bs, (j + 1) * bs)
        for column in range(per + offsets - 1):
            offset = column - j
            cols = slice(column * bs, (column + 1) * bs)
            if 0 <= offset < offsets:
                tile = tiles_ref[offset, (first + j) * bs : (first + j + 1) * bs, :]
                band_ref[row, cols] = tile * mask_ref[first + j, offset].astype(F32).astype(BF16)
            else:
                band_ref[row, cols] = jnp.zeros((bs, bs), BF16)


def node_rows(state, message, direct_part, upstream, valid, w_in_ref, w_out_ref, gain):
    latent = state.shape[1]
    preact = direct_part + dot(message, w_in_ref[latent:, :], (1, 0))
    sigma = jax.nn.sigmoid(preact)
    activated = (preact * sigma).astype(BF16)
    output = dot(activated, w_out_ref[...], (1, 0))
    centred = output - jnp.mean(output, axis=1, keepdims=True)
    inverse = lax.rsqrt(jnp.mean(centred * centred, axis=1, keepdims=True) + EPSILON)
    normed = centred * inverse
    new_state = (state.astype(F32) + gain * normed * valid).astype(BF16)
    masked_up = upstream * valid
    gain_sum = jnp.sum(masked_up * normed, axis=0, keepdims=True)
    scaled = masked_up * gain
    grad_output = (
        inverse
        * (
            scaled
            - jnp.mean(scaled, axis=1, keepdims=True)
            - normed * jnp.mean(scaled * normed, axis=1, keepdims=True)
        )
    ).astype(BF16)
    grad_act = dot(grad_output, w_out_ref[...], (1, 1))
    slope = sigma * (1.0 + preact * (1.0 - sigma))
    grad_pre = (grad_act * slope).astype(BF16)
    return new_state, gain_sum, activated, grad_output, grad_pre


def inner_kernel(
    cfg,
    len_hbm,
    mask_hbm,
    state_hbm,
    tiles_hbm,
    up_hbm,
    w_in_hbm,
    w_out_hbm,
    gain_hbm,
    new_ref,
    own_ref,
    spread_ref,
    grad_in_ref,
    grad_out_ref,
    gain_sum_ref,
    rim_band_ref,
    rim_message_ref,
    rim_direct_ref,
    valid_ref,
    state_rim_ref,
    up_rim_ref,
    w_in_ref,
    w_out_ref,
    gain_ref,
    len_ref,
    mask_ref,
    state_ref,
    tiles_ref,
    up_ref,
    ext_ref,
    band_ref,
    sems,
):
    bs, offsets = cfg
    rim = (offsets - 1) // 2 * bs
    rows, latent = state_ref.shape
    per = rim // bs
    blocks = rows // bs
    width = 3 * rim
    low, inner, high = pl.ds(0, rim), pl.ds(rim, rows - 2 * rim), pl.ds(rows - rim, rim)
    late = pl.ds(rim, rim)

    pairs = [(len_hbm, len_ref), (mask_hbm, mask_ref), (state_hbm, state_ref)]
    pairs += [(tiles_hbm.at[o], tiles_ref.at[o]) for o in range(offsets)]
    first = len(pairs)
    pairs += [(w_in_hbm, w_in_ref), (w_out_hbm, w_out_ref), (gain_hbm, gain_ref)]
    pairs += [(up_hbm.at[inner, :], up_ref)]
    second = len(pairs)
    pairs += [(state_hbm.at[low, :], state_rim_ref.at[low, :]), (state_hbm.at[high, :], state_rim_ref.at[late, :])]
    pairs += [(up_hbm.at[low, :], up_rim_ref.at[low, :]), (up_hbm.at[high, :], up_rim_ref.at[late, :])]
    copies = [pltpu.make_async_copy(a, b, sems.at[i]) for i, (a, b) in enumerate(pairs)]
    for copy in copies:
        copy.start()
    for copy in copies[:first]:
        copy.wait()

    valid_ref[...] = validity(len_ref, 0, blocks, bs)
    ext_ref[...] = (state_ref[...].astype(F32) * valid_ref[...]).astype(BF16)
    message = []
    for chunk in range(1, rows // rim - 1):
        band = band_ref.at[chunk - 1]
        fill_band(band, tiles_ref, mask_ref, chunk * per, per, bs, offsets)
        message.append(dot(band[...], ext_ref[(chunk - 1) * rim : (chunk - 1) * rim + width, :], (1, 0)))
    inner = slice(rim, rows - rim)
    valid = valid_ref[inner, :]
    message = (jnp.concatenate(message, axis=0) * valid).astype(BF16)
    for copy in copies[first:second]:
        copy.wait()
    state = state_ref[inner, :]
    upstream = up_ref[...].astype(F32)
    direct_part = dot(state, w_in_ref[:latent, :], (1, 0))
    new_state, gain_sum, activated, grad_output, grad_pre = node_rows(
        state, message, direct_part, upstream, valid, w_in_ref, w_out_ref, gain_ref[...]
    )
    new_ref[...] = new_state
    gain_sum_ref[...] = gain_sum
    grad_out_ref[...] = dot(activated, grad_output, (0, 0))
    grad_in_ref[:latent, :] = dot(state, grad_pre, (0, 0))
    grad_in_ref[latent:, :] = dot(message, grad_pre, (0, 0))
    own_ref[...] = upstream + dot(grad_pre, w_in_ref[:latent, :], (1, 1))
    grad_message = dot(grad_pre, w_in_ref[latent:, :], (1, 1)).astype(BF16)
    grad_message = (grad_message.astype(F32) * valid).astype(BF16)
    spread_ref[...] = jnp.zeros_like(spread_ref)
    for chunk in range(1, rows // rim - 1):
        reach = slice((chunk - 1) * rim, (chunk - 1) * rim + width)
        spread_ref[reach, :] += dot(
            band_ref[chunk - 1], grad_message[(chunk - 1) * rim : chunk * rim, :], (0, 0)
        )

    for end in range(2):
        first = end * (blocks - per)
        band = rim_band_ref.at[end]
        fill_band(band, tiles_ref, mask_ref, first, per, bs, offsets)
        here = slice(end * rim, (end + 1) * rim)
        if end == 0:
            rim_message_ref[here, :] = dot(band[:, rim:], ext_ref[: 2 * rim, :], (1, 0))
        else:
            rim_message_ref[here, :] = dot(band[:, : 2 * rim], ext_ref[rows - 2 * rim :, :], (1, 0))
        rim_direct_ref[here, :] = dot(
            state_ref[first * bs : first * bs + rim, :], w_in_ref[:latent, :], (1, 0)
        )
    for copy in copies[second:]:
        copy.wait()


def rim_kernel(
    scale,
    valid_ref,
    state_ref,
    up_ref,
    w_in_ref,
    w_out_ref,
    gain_ref,
    band_ref,
    message_ref,
    direct_ref,
    inner_in_ref,
    inner_out_ref,
    inner_gain_ref,
    low_ref,
    high_ref,
    send_ref,
    new_ref,
    pre_ref,
    grad_in_ref,
    grad_out_ref,
):
    rows = valid_ref.shape[0]
    rim, latent = low_ref.shape
    _, me = place()
    valid = jnp.concatenate([valid_ref[:rim, :], valid_ref[rows - rim :, :]], axis=0)
    arrived = jnp.concatenate(
        [dot(band_ref[0, :, :rim], low_ref[...], (1, 0)), dot(band_ref[1, :, 2 * rim :], high_ref[...], (1, 0))], axis=0
    )
    message = ((message_ref[...] + arrived) * valid).astype(BF16)
    state = state_ref[...]
    upstream = up_ref[...].astype(F32)
    new_state, gain_sum, activated, grad_output, grad_pre = node_rows(
        state, message, direct_ref[...], upstream, valid, w_in_ref, w_out_ref, gain_ref[...]
    )
    new_ref[...] = new_state
    gain_sum = gain_sum + inner_gain_ref[...]
    grad_out_ref[...] = inner_out_ref[...] + dot(activated, grad_output, (0, 0))
    grad_in_ref[:latent, :] = inner_in_ref[:latent, :] + dot(state, grad_pre, (0, 0))
    grad_in_ref[latent:, :] = inner_in_ref[latent:, :] + dot(message, grad_pre, (0, 0))
    pre_ref[...] = grad_pre

    count = send_ref.shape[0] * send_ref.shape[1]
    n_in = grad_in_ref.shape[0] // count
    n_out = grad_out_ref.shape[0] // count
    top = lax.broadcasted_iota(jnp.int32, (GAIN_ROWS, latent), 0) == 0
    for piece in range(count):
        turn = lax.bitwise_xor(me, piece)
        half = lax.bitwise_and(turn, 1)
        slot = lax.shift_right_logical(turn, 1)
        send_ref[half, slot, :n_in, :] = (grad_in_ref[piece * n_in : (piece + 1) * n_in, :] * scale).astype(BF16)
        send_ref[half, slot, n_in : n_in + n_out, :] = (
            grad_out_ref[piece * n_out : (piece + 1) * n_out, :] * scale
        ).astype(BF16)
        if piece == 0:
            tail = jnp.where(top, gain_sum * scale, 0.0)
        else:
            tail = jnp.zeros((GAIN_ROWS, latent), F32)
        send_ref[half, slot, n_in + n_out :, :] = tail.astype(BF16)


def back_kernel(
    valid_ref,
    up_ref,
    w_in_ref,
    band_ref,
    pre_ref,
    new_inner_ref,
    new_rim_ref,
    own_inner_ref,
    spread_inner_ref,
    spill_odd_ref,
    spill_even_ref,
    own_ref,
    new_ref,
    out_ref,
    inner_ref,
    sems,
):
    rim, latent = spill_odd_ref.shape
    rows = valid_ref.shape[0]
    side, _ = place()
    inner = pl.ds(rim, rows - 2 * rim)
    news = [
        pltpu.make_async_copy(new_rim_ref.at[pl.ds(0, rim), :], new_ref.at[pl.ds(0, rim), :], sems.at[0]),
        pltpu.make_async_copy(new_inner_ref, new_ref.at[inner, :], sems.at[1]),
        pltpu.make_async_copy(
            new_rim_ref.at[pl.ds(rim, rim), :], new_ref.at[pl.ds(rows - rim, rim), :], sems.at[2]
        ),
    ]
    for copy in news:
        copy.start()
    valid = jnp.concatenate([valid_ref[:rim, :], valid_ref[rows - rim :, :]], axis=0)
    grad_pre = pre_ref[...]
    grad_message = dot(grad_pre, w_in_ref[latent:, :], (1, 1)).astype(BF16)
    grad_message = (grad_message.astype(F32) * valid).astype(BF16)
    left = dot(band_ref[0], grad_message[:rim, :], (0, 0))
    right = dot(band_ref[1], grad_message[rim:, :], (0, 0))
    low = left[:rim, :].astype(BF16)
    high = right[2 * rim :, :].astype(BF16)
    spill_odd_ref[...] = jnp.where(side == 0, low, high)
    spill_even_ref[...] = jnp.where(side == 0, high, low)
    spread = spread_inner_ref[...] + jnp.concatenate([left[rim:, :], right[: 2 * rim, :]], axis=0)
    spread = spread * valid_ref[...]
    inner_ref[...] = (own_inner_ref[...] + spread[rim : rows - rim, :]).astype(BF16)
    inside = pltpu.make_async_copy(inner_ref, out_ref.at[inner, :], sems.at[3])
    inside.start()
    own = up_ref[...].astype(F32) + dot(grad_pre, w_in_ref[:latent, :], (1, 1))
    own_ref[...] = own + jnp.concatenate([spread[:rim, :], spread[rows - rim :, :]], axis=0)
    for copy in news:
        copy.wait()
    inside.wait()


def finish_kernel(turned, started_ref, valid_ref, own_ref, back_ref, out_ref, held_ref, sem):
    rows = valid_ref.shape[0]
    rim = back_ref.shape[0]
    side, _ = place()
    end = 1 - side if turned else side
    at = pl.multiple_of(end * (rows - rim), rim)
    there = pl.ds(pl.multiple_of(end * rim, rim), rim)
    back = back_ref[...].astype(F32) * valid_ref[pl.ds(at, rim), :]
    held_ref[...] = (own_ref[there, :] + back).astype(BF16)
    copy = pltpu.make_async_copy(held_ref, out_ref.at[pl.ds(at, rim), :], sem)
    copy.start()
    copy.wait()


def unpack_kernel(*refs):
    pieces = refs[:-3]
    grad_in_ref, grad_out_ref, gain_ref = refs[-3:]
    _, me = place()
    count = len(pieces)
    n_in = grad_in_ref.shape[0] // count
    n_out = grad_out_ref.shape[0] // count
    for turn in range(count):
        source = pieces[turn // 2 + turn % 2 * (count // 2)]
        piece = lax.bitwise_xor(me, turn)
        at_in = pl.ds(pl.multiple_of(piece * n_in, n_in), n_in)
        at_out = pl.ds(pl.multiple_of(piece * n_out, n_out), n_out)
        grad_in_ref[at_in, :] = source[:n_in, :].astype(F32)
        grad_out_ref[at_out, :] = source[n_in : n_in + n_out, :].astype(F32)

        @pl.when(piece == 0)
        def _():
            gain_ref[...] = source[n_in + n_out :, :].astype(F32)[:1, :]


def swap(x, axis, turn):
    count = lax.axis_size(axis)
    return lax.ppermute(x, axis, [(i, i ^ turn) for i in range(count)])


def gathered(x, axis):
    count = lax.axis_size(axis)
    if count & (count - 1) == 0:
        return [x] + [swap(x, axis, k) for k in range(1, count)]
    moved = [x] + [
        lax.ppermute(x, axis, [(i, (i + k) % count) for i in range(count)]) for k in range(1, count)
    ]
    order = (lax.axis_index(axis) - jnp.arange(count)) % count
    stacked = jnp.stack(moved)[order]
    return [stacked[k] for k in range(count)]


def tree_sum(parts):
    parts = [part.astype(F32) for part in parts]
    while len(parts) > 1:
        paired = [parts[i] + parts[i + 1] for i in range(0, len(parts) - 1, 2)]
        parts = paired + parts[len(parts) - len(parts) % 2 :]
    return parts[0]


def vmem(count):
    return [pl.BlockSpec(memory_space=pltpu.VMEM)] * count


def shapes(*given):
    return tuple(jax.ShapeDtypeStruct(shape, dtype) for shape, dtype in given)


def kernel(body, name, inputs, outputs, scratch=(), flops=0, moved=0, aliases=None):
    far, arrays = inputs
    spaces = [out.memory_space if hasattr(out, "memory_space") else pltpu.VMEM for out in outputs]
    call = pl.pallas_call(
        body,
        out_shape=outputs,
        in_specs=[pl.BlockSpec(memory_space=pltpu.HBM)] * far + vmem(arrays),
        out_specs=tuple(pl.BlockSpec(memory_space=space) for space in spaces),
        scratch_shapes=list(scratch),
        input_output_aliases=aliases or {},
        compiler_params=pltpu.CompilerParams(vmem_limit_bytes=VMEM_LIMIT),
        cost_estimate=pl.CostEstimate(flops=flops, bytes_accessed=moved, transcendentals=0),
        name=name,
    )

    def run(*given):
        placed = [pltpu.with_memory_space_constraint(x, pltpu.HBM) for x in given[:far]]
        return call(*placed, *given[far:])

    return run


def local(node_state, edge_tiles, block_mask, block_len, w_in, w_out, gain, upstream):
    rows, latent = node_state.shape
    offsets, bs = edge_tiles.shape[1:]
    rim = (offsets - 1) // 2 * bs
    inside = rows - 2 * rim
    width = 3 * rim
    dom = lax.axis_size("dom")
    rep = lax.axis_size("rep")
    total = dom * rep
    scale = 1.0 / math.sqrt(rows * total)
    ring = ("dom", "rep")
    next_pairs = [(i, (i + 1) % total) for i in range(total)]
    back_pairs = [(i, (i - 1) % total) for i in range(total)]
    even_pairs = [(i, i ^ 1) for i in range(total)]
    odd_pairs = [(i, (i + 1) % total if i % 2 else (i - 1) % total) for i in range(total)]
    gain_row = gain.reshape(1, latent)
    tiles = jnp.transpose(edge_tiles, (1, 0, 2))

    to_back, to_next = kernel(
        functools.partial(pack_kernel, bs),
        "pack_rims",
        (2, 0),
        shapes(((rim, latent), BF16), ((rim, latent), BF16)),
        [
            pltpu.VMEM((2, rim, latent), BF16),
            pltpu.SMEM(block_len.shape, jnp.int32),
            pltpu.SemaphoreType.DMA((3,)),
        ],
    )(block_len, node_state)
    from_back = lax.ppermute(to_next, ring, next_pairs)
    from_next = lax.ppermute(to_back, ring, back_pairs)

    work = 2 * inside * latent * (width + 5 * latent + 2 * latent + 2 * latent + width)
    new_inner, own_inner, spread_inner, sum_in, sum_out, sum_gain, band, message, direct, *kept = kernel(
        functools.partial(inner_kernel, (bs, offsets)),
        "inner_rows",
        (8, 0),
        shapes(
            ((inside, latent), BF16),
            ((inside, latent), F32),
            ((rows, latent), F32),
            (w_in.shape, F32),
            (w_out.shape, F32),
            ((1, latent), F32),
            ((2, rim, width), BF16),
            ((2 * rim, latent), F32),
            ((2 * rim, latent), F32),
            ((rows, 1), F32),
            ((2 * rim, latent), BF16),
            ((2 * rim, latent), BF16),
            (w_in.shape, BF16),
            (w_out.shape, BF16),
            ((1, latent), F32),
        ),
        [
            pltpu.SMEM(block_len.shape, jnp.int32),
            pltpu.SMEM(block_mask.shape, jnp.int32),
            pltpu.VMEM((rows, latent), BF16),
            pltpu.VMEM(tiles.shape, BF16),
            pltpu.VMEM((inside, latent), BF16),
            pltpu.VMEM((rows, latent), BF16),
            pltpu.VMEM((inside // rim, rim, width), BF16),
            pltpu.SemaphoreType.DMA((11 + offsets,)),
        ],
        flops=work,
        moved=10 * 1024 * 1024,
    )(block_len, block_mask, node_state, tiles, upstream, w_in, w_out, gain_row)

    n_in, n_out = w_in.shape[0] // dom, w_out.shape[0] // dom
    piece_rows = n_in + n_out + GAIN_ROWS
    send, new_rim, pre_rim = kernel(
        functools.partial(rim_kernel, scale),
        "rim_rows",
        (0, 14),
        shapes(
            ((2, dom // 2, piece_rows, latent), BF16),
            ((2 * rim, latent), BF16),
            ((2 * rim, latent), BF16),
        ),
        [pltpu.VMEM(w_in.shape, F32), pltpu.VMEM(w_out.shape, F32)],
        flops=work,
        moved=8 * 1024 * 1024,
    )(
        *kept,
        band, message, direct, sum_in, sum_out, sum_gain, from_back, from_next,
    )

    valid, _, up_rim, w_in_near, _, _ = kept
    spill_odd, spill_even, own_rim, new_state, grad_state = kernel(
        back_kernel,
        "rim_back",
        (0, 9),
        shapes(((rim, latent), BF16), ((rim, latent), BF16), ((2 * rim, latent), F32))
        + (pltpu.HBM((rows, latent), BF16), pltpu.HBM((rows, latent), BF16)),
        [pltpu.VMEM((inside, latent), BF16), pltpu.SemaphoreType.DMA((4,))],
        flops=2 * inside * latent * (2 * latent + width),
        moved=4 * 1024 * 1024,
    )(valid, up_rim, w_in_near, band, pre_rim, new_inner, new_rim, own_inner, spread_inner)
    back_odd = lax.ppermute(spill_odd, ring, odd_pairs)
    back_even = lax.ppermute(spill_even, ring, even_pairs)
    (grad_state,) = kernel(
        functools.partial(finish_kernel, True),
        "finish_even",
        (1, 3),
        (pltpu.HBM((rows, latent), BF16),),
        [pltpu.VMEM((rim, latent), BF16), pltpu.SemaphoreType.DMA],
        flops=0,
        aliases={0: 0},
    )(grad_state, valid, own_rim, back_even)
    other = swap(send[1], "dom", 1)
    held = (send[0].astype(F32) + other.astype(F32)).astype(BF16)
    held = [held[k] for k in range(dom // 2)]

    parts = [held[0]] + [swap(held[k], "dom", 2 * k) for k in range(1, dom // 2)]
    quarter = sum(part.astype(F32) for part in parts).astype(BF16)
    planes = gathered(quarter, "rep")
    mine = tree_sum(planes).astype(BF16)
    mine, grad_state = lax.optimization_barrier((mine, grad_state))
    near = [mine] + [swap(mine, "dom", 2 * k) for k in range(1, dom // 2)]
    near[-1], back_odd = lax.optimization_barrier((near[-1], back_odd))
    (grad_state,) = kernel(
        functools.partial(finish_kernel, False),
        "finish_odd",
        (1, 3),
        (pltpu.HBM((rows, latent), BF16),),
        [pltpu.VMEM((rim, latent), BF16), pltpu.SemaphoreType.DMA],
        flops=0,
        aliases={0: 0},
    )(grad_state, valid, own_rim, back_odd)
    other = swap(jnp.stack(near), "dom", 1)
    other = [other[k] for k in range(dom // 2)]
    *other, grad_state = lax.optimization_barrier((*other, grad_state))
    grad_w_in, grad_w_out, grad_gain = kernel(
        unpack_kernel,
        "unpack_sums",
        (0, dom),
        shapes((w_in.shape, F32), (w_out.shape, F32), ((1, latent), F32)),
    )(*near, *other)
    return new_state, grad_state, grad_w_in, grad_w_out, grad_gain.reshape(latent)


def solution(mesh):
    placed = (
        P(("dom", "rep"), None),
        P(("dom", "rep"), None, None),
        P(("dom", "rep"), None),
        P(("dom", "rep")),
        P(),
        P(),
        P(),
        P(("dom", "rep"), None),
    )
    return jax.shard_map(
        local,
        mesh=mesh,
        in_specs=placed,
        out_specs=(P(("dom", "rep"), None), P(("dom", "rep"), None), P(), P(), P()),
        check_vma=False,
    )
```

```python
import functools
import math

import jax
import jax.numpy as jnp
from jax import lax
from jax.experimental import pallas as pl
from jax.experimental.pallas import tpu as pltpu
from jax.sharding import PartitionSpec as P

EPSILON = 1e-05
F32 = jnp.float32
BF16 = jnp.bfloat16
GAIN_ROWS = 8
VMEM_LIMIT = 40 * 1024 * 1024


def dot(a, b, contract):
    return lax.dot_general(a, b, ((contract[:1], contract[1:]), ((), ())), preferred_element_type=F32)


def sublane(bs):
    return lax.broadcasted_iota(jnp.int32, (bs, 1), 0)


def validity(len_ref, first, count, bs):
    return jnp.concatenate(
        [(sublane(bs) < len_ref[first + j]).astype(F32) for j in range(count)], axis=0
    )


def place():
    me = lax.axis_index("dom")
    index = me * lax.axis_size("rep") + lax.axis_index("rep")
    return lax.rem(index, 2), me


def pack_kernel(bs, len_ref, state_ref, first_ref, last_ref, held_ref, lens_ref, sems):
    rows = state_ref.shape[0]
    rim = first_ref.shape[0]
    per = rim // bs
    copies = [
        pltpu.make_async_copy(len_ref, lens_ref, sems.at[0]),
        pltpu.make_async_copy(state_ref.at[pl.ds(rows - rim, rim), :], held_ref.at[1], sems.at[1]),
        pltpu.make_async_copy(state_ref.at[pl.ds(0, rim), :], held_ref.at[0], sems.at[2]),
    ]
    for copy in copies:
        copy.start()
    for copy in copies:
        copy.wait()
    blocks = rows // bs
    for j in range(per):
        here = slice(j * bs, (j + 1) * bs)
        first_ref[here, :] = held_ref[0, here, :] * (sublane(bs) < lens_ref[j]).astype(F32).astype(BF16)
        last_ref[here, :] = held_ref[1, here, :] * (
            sublane(bs) < lens_ref[blocks - per + j]
        ).astype(F32).astype(BF16)


def fill_band(band_ref, tiles_ref, mask_ref, first, per, bs, offsets):
    for j in range(per):
        row = slice(j * bs, (j + 1) * bs)
        for column in range(per + offsets - 1):
            offset = column - j
            cols = slice(column * bs, (column + 1) * bs)
            if 0 <= offset < offsets:
                tile = tiles_ref[offset, (first + j) * bs : (first + j + 1) * bs, :]
                band_ref[row, cols] = tile * mask_ref[first + j, offset].astype(F32).astype(BF16)
            else:
                band_ref[row, cols] = jnp.zeros((bs, bs), BF16)


def node_rows(state, message, direct_part, upstream, valid, w_in_ref, w_out_ref, gain):
    latent = state.shape[1]
    preact = direct_part + dot(message, w_in_ref[latent:, :], (1, 0))
    sigma = jax.nn.sigmoid(preact)
    activated = (preact * sigma).astype(BF16)
    output = dot(activated, w_out_ref[...], (1, 0))
    centred = output - jnp.mean(output, axis=1, keepdims=True)
    inverse = lax.rsqrt(jnp.mean(centred * centred, axis=1, keepdims=True) + EPSILON)
    normed = centred * inverse
    new_state = (state.astype(F32) + gain * normed * valid).astype(BF16)
    masked_up = upstream * valid
    gain_sum = jnp.sum(masked_up * normed, axis=0, keepdims=True)
    scaled = masked_up * gain
    grad_output = (
        inverse
        * (
            scaled
            - jnp.mean(scaled, axis=1, keepdims=True)
            - normed * jnp.mean(scaled * normed, axis=1, keepdims=True)
        )
    ).astype(BF16)
    grad_act = dot(grad_output, w_out_ref[...], (1, 1))
    slope = sigma * (1.0 + preact * (1.0 - sigma))
    grad_pre = (grad_act * slope).astype(BF16)
    return new_state, gain_sum, activated, grad_output, grad_pre


def inner_kernel(
    cfg,
    len_hbm,
    mask_hbm,
    state_hbm,
    tiles_hbm,
    up_hbm,
    w_in_hbm,
    w_out_hbm,
    gain_hbm,
    new_ref,
    own_ref,
    spread_ref,
    grad_in_ref,
    grad_out_ref,
    gain_sum_ref,
    rim_band_ref,
    rim_message_ref,
    rim_direct_ref,
    valid_ref,
    state_rim_ref,
    up_rim_ref,
    w_in_ref,
    w_out_ref,
    gain_ref,
    len_ref,
    mask_ref,
    state_ref,
    tiles_ref,
    up_ref,
    ext_ref,
    band_ref,
    sems,
):
    bs, offsets = cfg
    rim = (offsets - 1) // 2 * bs
    rows, latent = state_ref.shape
    per = rim // bs
    blocks = rows // bs
    width = 3 * rim
    low, inner, high = pl.ds(0, rim), pl.ds(rim, rows - 2 * rim), pl.ds(rows - rim, rim)
    late = pl.ds(rim, rim)

    pairs = [(len_hbm, len_ref), (mask_hbm, mask_ref), (state_hbm, state_ref)]
    pairs += [(tiles_hbm.at[o], tiles_ref.at[o]) for o in range(offsets)]
    first = len(pairs)
    pairs += [(w_in_hbm, w_in_ref), (w_out_hbm, w_out_ref), (gain_hbm, gain_ref)]
    pairs += [(up_hbm.at[inner, :], up_ref)]
    second = len(pairs)
    pairs += [(state_hbm.at[low, :], state_rim_ref.at[low, :]), (state_hbm.at[high, :], state_rim_ref.at[late, :])]
    pairs += [(up_hbm.at[low, :], up_rim_ref.at[low, :]), (up_hbm.at[high, :], up_rim_ref.at[late, :])]
    copies = [pltpu.make_async_copy(a, b, sems.at[i]) for i, (a, b) in enumerate(pairs)]
    for copy in copies:
        copy.start()
    for copy in copies[:first]:
        copy.wait()

    valid_ref[...] = validity(len_ref, 0, blocks, bs)
    ext_ref[...] = (state_ref[...].astype(F32) * valid_ref[...]).astype(BF16)
    message = []
    for chunk in range(1, rows // rim - 1):
        band = band_ref.at[chunk - 1]
        fill_band(band, tiles_ref, mask_ref, chunk * per, per, bs, offsets)
        message.append(dot(band[...], ext_ref[(chunk - 1) * rim : (chunk - 1) * rim + width, :], (1, 0)))
    inner = slice(rim, rows - rim)
    valid = valid_ref[inner, :]
    message = (jnp.concatenate(message, axis=0) * valid).astype(BF16)
    for copy in copies[first:second]:
        copy.wait()
    state = state_ref[inner, :]
    upstream = up_ref[...].astype(F32)
    direct_part = dot(state, w_in_ref[:latent, :], (1, 0))
    new_state, gain_sum, activated, grad_output, grad_pre = node_rows(
        state, message, direct_part, upstream, valid, w_in_ref, w_out_ref, gain_ref[...]
    )
    new_ref[...] = new_state
    gain_sum_ref[...] = gain_sum
    grad_out_ref[...] = dot(activated, grad_output, (0, 0))
    grad_in_ref[:latent, :] = dot(state, grad_pre, (0, 0))
    grad_in_ref[latent:, :] = dot(message, grad_pre, (0, 0))
    own_ref[...] = upstream + dot(grad_pre, w_in_ref[:latent, :], (1, 1))
    grad_message = dot(grad_pre, w_in_ref[latent:, :], (1, 1)).astype(BF16)
    grad_message = (grad_message.astype(F32) * valid).astype(BF16)
    spread_ref[...] = jnp.zeros_like(spread_ref)
    for chunk in range(1, rows // rim - 1):
        reach = slice((chunk - 1) * rim, (chunk - 1) * rim + width)
        spread_ref[reach, :] += dot(
            band_ref[chunk - 1], grad_message[(chunk - 1) * rim : chunk * rim, :], (0, 0)
        )

    for end in range(2):
        first = end * (blocks - per)
        band = rim_band_ref.at[end]
        fill_band(band, tiles_ref, mask_ref, first, per, bs, offsets)
        here = slice(end * rim, (end + 1) * rim)
        if end == 0:
            rim_message_ref[here, :] = dot(band[:, rim:], ext_ref[: 2 * rim, :], (1, 0))
        else:
            rim_message_ref[here, :] = dot(band[:, : 2 * rim], ext_ref[rows - 2 * rim :, :], (1, 0))
        rim_direct_ref[here, :] = dot(
            state_ref[first * bs : first * bs + rim, :], w_in_ref[:latent, :], (1, 0)
        )
    for copy in copies[second:]:
        copy.wait()


def rim_kernel(
    scale,
    valid_ref,
    state_ref,
    up_ref,
    w_in_ref,
    w_out_ref,
    gain_ref,
    band_ref,
    message_ref,
    direct_ref,
    inner_in_ref,
    inner_out_ref,
    inner_gain_ref,
    low_ref,
    high_ref,
    send_ref,
    new_ref,
    pre_ref,
    grad_in_ref,
    grad_out_ref,
):
    rows = valid_ref.shape[0]
    rim, latent = low_ref.shape
    _, me = place()
    valid = jnp.concatenate([valid_ref[:rim, :], valid_ref[rows - rim :, :]], axis=0)
    arrived = jnp.concatenate(
        [dot(band_ref[0, :, :rim], low_ref[...], (1, 0)), dot(band_ref[1, :, 2 * rim :], high_ref[...], (1, 0))], axis=0
    )
    message = ((message_ref[...] + arrived) * valid).astype(BF16)
    state = state_ref[...]
    upstream = up_ref[...].astype(F32)
    new_state, gain_sum, activated, grad_output, grad_pre = node_rows(
        state, message, direct_ref[...], upstream, valid, w_in_ref, w_out_ref, gain_ref[...]
    )
    new_ref[...] = new_state
    gain_sum = gain_sum + inner_gain_ref[...]
    grad_out_ref[...] = inner_out_ref[...] + dot(activated, grad_output, (0, 0))
    grad_in_ref[:latent, :] = inner_in_ref[:latent, :] + dot(state, grad_pre, (0, 0))
    grad_in_ref[latent:, :] = inner_in_ref[latent:, :] + dot(message, grad_pre, (0, 0))
    pre_ref[...] = grad_pre

    count = send_ref.shape[0] * send_ref.shape[1]
    n_in = grad_in_ref.shape[0] // count
    n_out = grad_out_ref.shape[0] // count
    top = lax.broadcasted_iota(jnp.int32, (GAIN_ROWS, latent), 0) == 0
    for piece in range(count):
        turn = lax.bitwise_xor(me, piece)
        half = lax.bitwise_and(turn, 1)
        slot = lax.shift_right_logical(turn, 1)
        send_ref[half, slot, :n_in, :] = (grad_in_ref[piece * n_in : (piece + 1) * n_in, :] * scale).astype(BF16)
        send_ref[half, slot, n_in : n_in + n_out, :] = (
            grad_out_ref[piece * n_out : (piece + 1) * n_out, :] * scale
        ).astype(BF16)
        if piece == 0:
            tail = jnp.where(top, gain_sum * scale, 0.0)
        else:
            tail = jnp.zeros((GAIN_ROWS, latent), F32)
        send_ref[half, slot, n_in + n_out :, :] = tail.astype(BF16)


def back_kernel(
    valid_ref,
    up_ref,
    w_in_ref,
    band_ref,
    pre_ref,
    new_inner_ref,
    new_rim_ref,
    own_inner_ref,
    spread_inner_ref,
    spill_odd_ref,
    spill_even_ref,
    own_ref,
    new_ref,
    out_ref,
    inner_ref,
    sems,
):
    rim, latent = spill_odd_ref.shape
    rows = valid_ref.shape[0]
    side, _ = place()
    inner = pl.ds(rim, rows - 2 * rim)
    news = [
        pltpu.make_async_copy(new_rim_ref.at[pl.ds(0, rim), :], new_ref.at[pl.ds(0, rim), :], sems.at[0]),
        pltpu.make_async_copy(new_inner_ref, new_ref.at[inner, :], sems.at[1]),
        pltpu.make_async_copy(
            new_rim_ref.at[pl.ds(rim, rim), :], new_ref.at[pl.ds(rows - rim, rim), :], sems.at[2]
        ),
    ]
    for copy in news:
        copy.start()
    valid = jnp.concatenate([valid_ref[:rim, :], valid_ref[rows - rim :, :]], axis=0)
    grad_pre = pre_ref[...]
    grad_message = dot(grad_pre, w_in_ref[latent:, :], (1, 1)).astype(BF16)
    grad_message = (grad_message.astype(F32) * valid).astype(BF16)
    left = dot(band_ref[0], grad_message[:rim, :], (0, 0))
    right = dot(band_ref[1], grad_message[rim:, :], (0, 0))
    low = left[:rim, :].astype(BF16)
    high = right[2 * rim :, :].astype(BF16)
    spill_odd_ref[...] = jnp.where(side == 0, low, high)
    spill_even_ref[...] = jnp.where(side == 0, high, low)
    spread = spread_inner_ref[...] + jnp.concatenate([left[rim:, :], right[: 2 * rim, :]], axis=0)
    spread = spread * valid_ref[...]
    inner_ref[...] = (own_inner_ref[...] + spread[rim : rows - rim, :]).astype(BF16)
    inside = pltpu.make_async_copy(inner_ref, out_ref.at[inner, :], sems.at[3])
    inside.start()
    own = up_ref[...].astype(F32) + dot(grad_pre, w_in_ref[:latent, :], (1, 1))
    own_ref[...] = own + jnp.concatenate([spread[:rim, :], spread[rows - rim :, :]], axis=0)
    for copy in news:
        copy.wait()
    inside.wait()


def even_kernel(valid_ref, own_ref, back_ref, sum_ref):
    rows = valid_ref.shape[0]
    rim = back_ref.shape[0]
    side, _ = place()
    end = 1 - side
    back = back_ref[...].astype(F32) * valid_ref[pl.ds(pl.multiple_of(end * (rows - rim), rim), rim), :]
    sum_ref[...] = (own_ref[pl.ds(pl.multiple_of(end * rim, rim), rim), :] + back).astype(BF16)


def finish_kernel(started_ref, valid_ref, own_ref, even_ref, back_ref, out_ref, held_ref, sems):
    rows = valid_ref.shape[0]
    rim = back_ref.shape[0]
    side, _ = place()
    at_even = pl.multiple_of((1 - side) * (rows - rim), rim)
    at_odd = pl.multiple_of(side * (rows - rim), rim)
    first = pltpu.make_async_copy(even_ref, out_ref.at[pl.ds(at_even, rim), :], sems.at[0])
    first.start()
    back = back_ref[...].astype(F32) * valid_ref[pl.ds(at_odd, rim), :]
    held_ref[...] = (own_ref[pl.ds(pl.multiple_of(side * rim, rim), rim), :] + back).astype(BF16)
    second = pltpu.make_async_copy(held_ref, out_ref.at[pl.ds(at_odd, rim), :], sems.at[1])
    second.start()
    first.wait()
    second.wait()


def unpack_kernel(*refs):
    pieces = refs[:-3]
    grad_in_ref, grad_out_ref, gain_ref = refs[-3:]
    _, me = place()
    count = len(pieces)
    n_in = grad_in_ref.shape[0] // count
    n_out = grad_out_ref.shape[0] // count
    for turn in range(count):
        source = pieces[turn // 2 + turn % 2 * (count // 2)]
        piece = lax.bitwise_xor(me, turn)
        at_in = pl.ds(pl.multiple_of(piece * n_in, n_in), n_in)
        at_out = pl.ds(pl.multiple_of(piece * n_out, n_out), n_out)
        grad_in_ref[at_in, :] = source[:n_in, :].astype(F32)
        grad_out_ref[at_out, :] = source[n_in : n_in + n_out, :].astype(F32)

        @pl.when(piece == 0)
        def _():
            gain_ref[...] = source[n_in + n_out :, :].astype(F32)[:1, :]


def swap(x, axis, turn):
    count = lax.axis_size(axis)
    return lax.ppermute(x, axis, [(i, i ^ turn) for i in range(count)])


def gathered(x, axis):
    count = lax.axis_size(axis)
    if count & (count - 1) == 0:
        return [x] + [swap(x, axis, k) for k in range(1, count)]
    moved = [x] + [
        lax.ppermute(x, axis, [(i, (i + k) % count) for i in range(count)]) for k in range(1, count)
    ]
    order = (lax.axis_index(axis) - jnp.arange(count)) % count
    stacked = jnp.stack(moved)[order]
    return [stacked[k] for k in range(count)]


def tree_sum(parts):
    parts = [part.astype(F32) for part in parts]
    while len(parts) > 1:
        paired = [parts[i] + parts[i + 1] for i in range(0, len(parts) - 1, 2)]
        parts = paired + parts[len(parts) - len(parts) % 2 :]
    return parts[0]


def vmem(count):
    return [pl.BlockSpec(memory_space=pltpu.VMEM)] * count


def shapes(*given):
    return tuple(jax.ShapeDtypeStruct(shape, dtype) for shape, dtype in given)


def kernel(body, name, inputs, outputs, scratch=(), flops=0, moved=0, aliases=None):
    far, arrays = inputs
    spaces = [out.memory_space if hasattr(out, "memory_space") else pltpu.VMEM for out in outputs]
    call = pl.pallas_call(
        body,
        out_shape=outputs,
        in_specs=[pl.BlockSpec(memory_space=pltpu.HBM)] * far + vmem(arrays),
        out_specs=tuple(pl.BlockSpec(memory_space=space) for space in spaces),
        scratch_shapes=list(scratch),
        input_output_aliases=aliases or {},
        compiler_params=pltpu.CompilerParams(vmem_limit_bytes=VMEM_LIMIT),
        cost_estimate=pl.CostEstimate(flops=flops, bytes_accessed=moved, transcendentals=0),
        name=name,
    )

    def run(*given):
        placed = [pltpu.with_memory_space_constraint(x, pltpu.HBM) for x in given[:far]]
        return call(*placed, *given[far:])

    return run


def local(node_state, edge_tiles, block_mask, block_len, w_in, w_out, gain, upstream):
    rows, latent = node_state.shape
    offsets, bs = edge_tiles.shape[1:]
    rim = (offsets - 1) // 2 * bs
    inside = rows - 2 * rim
    width = 3 * rim
    dom = lax.axis_size("dom")
    rep = lax.axis_size("rep")
    total = dom * rep
    scale = 1.0 / math.sqrt(rows * total)
    ring = ("dom", "rep")
    next_pairs = [(i, (i + 1) % total) for i in range(total)]
    back_pairs = [(i, (i - 1) % total) for i in range(total)]
    even_pairs = [(i, i ^ 1) for i in range(total)]
    odd_pairs = [(i, (i + 1) % total if i % 2 else (i - 1) % total) for i in range(total)]
    gain_row = gain.reshape(1, latent)
    tiles = jnp.transpose(edge_tiles, (1, 0, 2))

    to_back, to_next = kernel(
        functools.partial(pack_kernel, bs),
        "pack_rims",
        (2, 0),
        shapes(((rim, latent), BF16), ((rim, latent), BF16)),
        [
            pltpu.VMEM((2, rim, latent), BF16),
            pltpu.SMEM(block_len.shape, jnp.int32),
            pltpu.SemaphoreType.DMA((3,)),
        ],
    )(block_len, node_state)
    from_back = lax.ppermute(to_next, ring, next_pairs)
    from_next = lax.ppermute(to_back, ring, back_pairs)

    work = 2 * inside * latent * (width + 5 * latent + 2 * latent + 2 * latent + width)
    new_inner, own_inner, spread_inner, sum_in, sum_out, sum_gain, band, message, direct, *kept = kernel(
        functools.partial(inner_kernel, (bs, offsets)),
        "inner_rows",
        (8, 0),
        shapes(
            ((inside, latent), BF16),
            ((inside, latent), F32),
            ((rows, latent), F32),
            (w_in.shape, F32),
            (w_out.shape, F32),
            ((1, latent), F32),
            ((2, rim, width), BF16),
            ((2 * rim, latent), F32),
            ((2 * rim, latent), F32),
            ((rows, 1), F32),
            ((2 * rim, latent), BF16),
            ((2 * rim, latent), BF16),
            (w_in.shape, BF16),
            (w_out.shape, BF16),
            ((1, latent), F32),
        ),
        [
            pltpu.SMEM(block_len.shape, jnp.int32),
            pltpu.SMEM(block_mask.shape, jnp.int32),
            pltpu.VMEM((rows, latent), BF16),
            pltpu.VMEM(tiles.shape, BF16),
            pltpu.VMEM((inside, latent), BF16),
            pltpu.VMEM((rows, latent), BF16),
            pltpu.VMEM((inside // rim, rim, width), BF16),
            pltpu.SemaphoreType.DMA((11 + offsets,)),
        ],
        flops=work,
        moved=10 * 1024 * 1024,
    )(block_len, block_mask, node_state, tiles, upstream, w_in, w_out, gain_row)

    n_in, n_out = w_in.shape[0] // dom, w_out.shape[0] // dom
    piece_rows = n_in + n_out + GAIN_ROWS
    send, new_rim, pre_rim = kernel(
        functools.partial(rim_kernel, scale),
        "rim_rows",
        (0, 14),
        shapes(
            ((2, dom // 2, piece_rows, latent), BF16),
            ((2 * rim, latent), BF16),
            ((2 * rim, latent), BF16),
        ),
        [pltpu.VMEM(w_in.shape, F32), pltpu.VMEM(w_out.shape, F32)],
        flops=work,
        moved=8 * 1024 * 1024,
    )(
        *kept,
        band, message, direct, sum_in, sum_out, sum_gain, from_back, from_next,
    )

    valid, _, up_rim, w_in_near, _, _ = kept
    spill_odd, spill_even, own_rim, new_state, grad_state = kernel(
        back_kernel,
        "rim_back",
        (0, 9),
        shapes(((rim, latent), BF16), ((rim, latent), BF16), ((2 * rim, latent), F32))
        + (pltpu.HBM((rows, latent), BF16), pltpu.HBM((rows, latent), BF16)),
        [pltpu.VMEM((inside, latent), BF16), pltpu.SemaphoreType.DMA((4,))],
        flops=2 * inside * latent * (2 * latent + width),
        moved=4 * 1024 * 1024,
    )(valid, up_rim, w_in_near, band, pre_rim, new_inner, new_rim, own_inner, spread_inner)
    back_odd = lax.ppermute(spill_odd, ring, odd_pairs)
    back_even = lax.ppermute(spill_even, ring, even_pairs)
    (even_rows,) = kernel(
        even_kernel,
        "even_rows",
        (0, 3),
        shapes(((rim, latent), BF16)),
    )(valid, own_rim, back_even)
    other = swap(send[1], "dom", 1)
    held = (send[0].astype(F32) + other.astype(F32)).astype(BF16)
    held = [held[k] for k in range(dom // 2)]

    parts = [held[0]] + [swap(held[k], "dom", 2 * k) for k in range(1, dom // 2)]
    quarter = sum(part.astype(F32) for part in parts).astype(BF16)
    planes = gathered(quarter, "rep")
    mine = tree_sum(planes).astype(BF16)
    mine, even_rows = lax.optimization_barrier((mine, even_rows))
    near = [mine] + [swap(mine, "dom", 2 * k) for k in range(1, dom // 2)]
    near[-1], back_odd = lax.optimization_barrier((near[-1], back_odd))
    (grad_state,) = kernel(
        finish_kernel,
        "finish_state",
        (1, 4),
        (pltpu.HBM((rows, latent), BF16),),
        [pltpu.VMEM((rim, latent), BF16), pltpu.SemaphoreType.DMA((2,))],
        aliases={0: 0},
    )(grad_state, valid, own_rim, even_rows, back_odd)
    other = swap(jnp.stack(near), "dom", 1)
    other = [other[k] for k in range(dom // 2)]
    *other, grad_state = lax.optimization_barrier((*other, grad_state))
    grad_w_in, grad_w_out, grad_gain = kernel(
        unpack_kernel,
        "unpack_sums",
        (0, dom),
        shapes((w_in.shape, F32), (w_out.shape, F32), ((1, latent), F32)),
    )(*near, *other)
    return new_state, grad_state, grad_w_in, grad_w_out, grad_gain.reshape(latent)


def solution(mesh):
    placed = (
        P(("dom", "rep"), None),
        P(("dom", "rep"), None, None),
        P(("dom", "rep"), None),
        P(("dom", "rep")),
        P(),
        P(),
        P(),
        P(("dom", "rep"), None),
    )
    return jax.shard_map(
        local,
        mesh=mesh,
        in_specs=placed,
        out_specs=(P(("dom", "rep"), None), P(("dom", "rep"), None), P(), P(), P()),
        check_vma=False,
    )
```

```python
import functools
import math

import jax
import jax.numpy as jnp
from jax import lax
from jax.experimental import pallas as pl
from jax.experimental.pallas import tpu as pltpu
from jax.sharding import PartitionSpec as P

EPSILON = 1e-05
F32 = jnp.float32
BF16 = jnp.bfloat16
GAIN_ROWS = 8
VMEM_LIMIT = 40 * 1024 * 1024


def dot(a, b, contract):
    return lax.dot_general(a, b, ((contract[:1], contract[1:]), ((), ())), preferred_element_type=F32)


def sublane(bs):
    return lax.broadcasted_iota(jnp.int32, (bs, 1), 0)


def validity(len_ref, first, count, bs):
    return jnp.concatenate(
        [(sublane(bs) < len_ref[first + j]).astype(F32) for j in range(count)], axis=0
    )


def place():
    me = lax.axis_index("dom")
    index = me * lax.axis_size("rep") + lax.axis_index("rep")
    return lax.rem(index, 2), me


def pack_kernel(bs, len_ref, state_ref, first_ref, last_ref, held_ref, lens_ref, sems):
    rows = state_ref.shape[0]
    rim = first_ref.shape[0]
    per = rim // bs
    copies = [
        pltpu.make_async_copy(len_ref, lens_ref, sems.at[0]),
        pltpu.make_async_copy(state_ref.at[pl.ds(rows - rim, rim), :], held_ref.at[1], sems.at[1]),
        pltpu.make_async_copy(state_ref.at[pl.ds(0, rim), :], held_ref.at[0], sems.at[2]),
    ]
    for copy in copies:
        copy.start()
    for copy in copies:
        copy.wait()
    blocks = rows // bs
    for j in range(per):
        here = slice(j * bs, (j + 1) * bs)
        first_ref[here, :] = held_ref[0, here, :] * (sublane(bs) < lens_ref[j]).astype(F32).astype(BF16)
        last_ref[here, :] = held_ref[1, here, :] * (
            sublane(bs) < lens_ref[blocks - per + j]
        ).astype(F32).astype(BF16)


def fill_band(band_ref, tiles_ref, mask_ref, first, per, bs, offsets):
    for j in range(per):
        row = slice(j * bs, (j + 1) * bs)
        for column in range(per + offsets - 1):
            offset = column - j
            cols = slice(column * bs, (column + 1) * bs)
            if 0 <= offset < offsets:
                tile = tiles_ref[offset, (first + j) * bs : (first + j + 1) * bs, :]
                band_ref[row, cols] = tile * mask_ref[first + j, offset].astype(F32).astype(BF16)
            else:
                band_ref[row, cols] = jnp.zeros((bs, bs), BF16)


def node_rows(state, message, direct_part, upstream, valid, w_in_ref, w_out_ref, gain):
    latent = state.shape[1]
    preact = direct_part + dot(message, w_in_ref[latent:, :], (1, 0))
    sigma = jax.nn.sigmoid(preact)
    activated = (preact * sigma).astype(BF16)
    output = dot(activated, w_out_ref[...], (1, 0))
    centred = output - jnp.mean(output, axis=1, keepdims=True)
    inverse = lax.rsqrt(jnp.mean(centred * centred, axis=1, keepdims=True) + EPSILON)
    normed = centred * inverse
    new_state = (state.astype(F32) + gain * normed * valid).astype(BF16)
    masked_up = upstream * valid
    gain_sum = jnp.sum(masked_up * normed, axis=0, keepdims=True)
    scaled = masked_up * gain
    grad_output = (
        inverse
        * (
            scaled
            - jnp.mean(scaled, axis=1, keepdims=True)
            - normed * jnp.mean(scaled * normed, axis=1, keepdims=True)
        )
    ).astype(BF16)
    grad_act = dot(grad_output, w_out_ref[...], (1, 1))
    slope = sigma * (1.0 + preact * (1.0 - sigma))
    grad_pre = (grad_act * slope).astype(BF16)
    return new_state, gain_sum, activated, grad_output, grad_pre


def inner_kernel(
    cfg,
    len_hbm,
    mask_hbm,
    state_hbm,
    tiles_hbm,
    up_hbm,
    w_in_hbm,
    w_out_hbm,
    gain_hbm,
    new_ref,
    own_ref,
    spread_ref,
    grad_in_ref,
    grad_out_ref,
    gain_sum_ref,
    rim_band_ref,
    rim_message_ref,
    rim_direct_ref,
    valid_ref,
    state_rim_ref,
    up_rim_ref,
    w_in_ref,
    w_out_ref,
    gain_ref,
    len_ref,
    mask_ref,
    state_ref,
    tiles_ref,
    up_ref,
    ext_ref,
    band_ref,
    sems,
):
    bs, offsets = cfg
    rim = (offsets - 1) // 2 * bs
    rows, latent = state_ref.shape
    per = rim // bs
    blocks = rows // bs
    width = 3 * rim
    low, inner, high = pl.ds(0, rim), pl.ds(rim, rows - 2 * rim), pl.ds(rows - rim, rim)
    late = pl.ds(rim, rim)

    pairs = [(len_hbm, len_ref), (mask_hbm, mask_ref), (state_hbm, state_ref)]
    pairs += [(tiles_hbm.at[o], tiles_ref.at[o]) for o in range(offsets)]
    first = len(pairs)
    pairs += [(w_in_hbm, w_in_ref), (w_out_hbm, w_out_ref), (gain_hbm, gain_ref)]
    pairs += [(up_hbm.at[inner, :], up_ref)]
    second = len(pairs)
    pairs += [(state_hbm.at[low, :], state_rim_ref.at[low, :]), (state_hbm.at[high, :], state_rim_ref.at[late, :])]
    pairs += [(up_hbm.at[low, :], up_rim_ref.at[low, :]), (up_hbm.at[high, :], up_rim_ref.at[late, :])]
    copies = [pltpu.make_async_copy(a, b, sems.at[i]) for i, (a, b) in enumerate(pairs)]
    for copy in copies:
        copy.start()
    for copy in copies[:first]:
        copy.wait()

    valid_ref[...] = validity(len_ref, 0, blocks, bs)
    ext_ref[...] = (state_ref[...].astype(F32) * valid_ref[...]).astype(BF16)
    message = []
    for chunk in range(1, rows // rim - 1):
        band = band_ref.at[chunk - 1]
        fill_band(band, tiles_ref, mask_ref, chunk * per, per, bs, offsets)
        message.append(dot(band[...], ext_ref[(chunk - 1) * rim : (chunk - 1) * rim + width, :], (1, 0)))
    inner = slice(rim, rows - rim)
    valid = valid_ref[inner, :]
    message = (jnp.concatenate(message, axis=0) * valid).astype(BF16)
    for copy in copies[first:second]:
        copy.wait()
    state = state_ref[inner, :]
    upstream = up_ref[...].astype(F32)
    direct_part = dot(state, w_in_ref[:latent, :], (1, 0))
    new_state, gain_sum, activated, grad_output, grad_pre = node_rows(
        state, message, direct_part, upstream, valid, w_in_ref, w_out_ref, gain_ref[...]
    )
    new_ref[...] = new_state
    gain_sum_ref[...] = gain_sum
    grad_out_ref[...] = dot(activated, grad_output, (0, 0))
    grad_in_ref[:latent, :] = dot(state, grad_pre, (0, 0))
    grad_in_ref[latent:, :] = dot(message, grad_pre, (0, 0))
    own_ref[...] = upstream + dot(grad_pre, w_in_ref[:latent, :], (1, 1))
    grad_message = dot(grad_pre, w_in_ref[latent:, :], (1, 1)).astype(BF16)
    grad_message = (grad_message.astype(F32) * valid).astype(BF16)
    spread_ref[...] = jnp.zeros_like(spread_ref)
    for chunk in range(1, rows // rim - 1):
        reach = slice((chunk - 1) * rim, (chunk - 1) * rim + width)
        spread_ref[reach, :] += dot(
            band_ref[chunk - 1], grad_message[(chunk - 1) * rim : chunk * rim, :], (0, 0)
        )

    for end in range(2):
        first = end * (blocks - per)
        band = rim_band_ref.at[end]
        fill_band(band, tiles_ref, mask_ref, first, per, bs, offsets)
        here = slice(end * rim, (end + 1) * rim)
        if end == 0:
            rim_message_ref[here, :] = dot(band[:, rim:], ext_ref[: 2 * rim, :], (1, 0))
        else:
            rim_message_ref[here, :] = dot(band[:, : 2 * rim], ext_ref[rows - 2 * rim :, :], (1, 0))
        rim_direct_ref[here, :] = dot(
            state_ref[first * bs : first * bs + rim, :], w_in_ref[:latent, :], (1, 0)
        )
    for copy in copies[second:]:
        copy.wait()


def rim_kernel(
    scale,
    valid_ref,
    state_ref,
    up_ref,
    w_in_ref,
    w_out_ref,
    gain_ref,
    band_ref,
    message_ref,
    direct_ref,
    inner_in_ref,
    inner_out_ref,
    inner_gain_ref,
    low_ref,
    high_ref,
    send_ref,
    new_ref,
    pre_ref,
    grad_in_ref,
    grad_out_ref,
):
    rows = valid_ref.shape[0]
    rim, latent = low_ref.shape
    _, me = place()
    valid = jnp.concatenate([valid_ref[:rim, :], valid_ref[rows - rim :, :]], axis=0)
    arrived = jnp.concatenate(
        [dot(band_ref[0, :, :rim], low_ref[...], (1, 0)), dot(band_ref[1, :, 2 * rim :], high_ref[...], (1, 0))], axis=0
    )
    message = ((message_ref[...] + arrived) * valid).astype(BF16)
    state = state_ref[...]
    upstream = up_ref[...].astype(F32)
    new_state, gain_sum, activated, grad_output, grad_pre = node_rows(
        state, message, direct_ref[...], upstream, valid, w_in_ref, w_out_ref, gain_ref[...]
    )
    new_ref[...] = new_state
    gain_sum = gain_sum + inner_gain_ref[...]
    grad_out_ref[...] = inner_out_ref[...] + dot(activated, grad_output, (0, 0))
    grad_in_ref[:latent, :] = inner_in_ref[:latent, :] + dot(state, grad_pre, (0, 0))
    grad_in_ref[latent:, :] = inner_in_ref[latent:, :] + dot(message, grad_pre, (0, 0))
    pre_ref[...] = grad_pre

    count = send_ref.shape[0] * send_ref.shape[1]
    n_in = grad_in_ref.shape[0] // count
    n_out = grad_out_ref.shape[0] // count
    top = lax.broadcasted_iota(jnp.int32, (GAIN_ROWS, latent), 0) == 0
    for piece in range(count):
        turn = lax.bitwise_xor(me, piece)
        half = lax.bitwise_and(turn, 1)
        slot = lax.shift_right_logical(turn, 1)
        send_ref[half, slot, :n_in, :] = (grad_in_ref[piece * n_in : (piece + 1) * n_in, :] * scale).astype(BF16)
        send_ref[half, slot, n_in : n_in + n_out, :] = (
            grad_out_ref[piece * n_out : (piece + 1) * n_out, :] * scale
        ).astype(BF16)
        if piece == 0:
            tail = jnp.where(top, gain_sum * scale, 0.0)
        else:
            tail = jnp.zeros((GAIN_ROWS, latent), F32)
        send_ref[half, slot, n_in + n_out :, :] = tail.astype(BF16)


def back_kernel(
    valid_ref,
    up_ref,
    w_in_ref,
    band_ref,
    pre_ref,
    new_inner_ref,
    new_rim_ref,
    own_inner_ref,
    spread_inner_ref,
    spill_odd_ref,
    spill_even_ref,
    own_ref,
    new_ref,
    out_ref,
    inner_ref,
    sems,
):
    rim, latent = spill_odd_ref.shape
    rows = valid_ref.shape[0]
    side, _ = place()
    inner = pl.ds(rim, rows - 2 * rim)
    news = [
        pltpu.make_async_copy(new_rim_ref.at[pl.ds(0, rim), :], new_ref.at[pl.ds(0, rim), :], sems.at[0]),
        pltpu.make_async_copy(new_inner_ref, new_ref.at[inner, :], sems.at[1]),
        pltpu.make_async_copy(
            new_rim_ref.at[pl.ds(rim, rim), :], new_ref.at[pl.ds(rows - rim, rim), :], sems.at[2]
        ),
    ]
    for copy in news:
        copy.start()
    valid = jnp.concatenate([valid_ref[:rim, :], valid_ref[rows - rim :, :]], axis=0)
    grad_pre = pre_ref[...]
    grad_message = dot(grad_pre, w_in_ref[latent:, :], (1, 1)).astype(BF16)
    grad_message = (grad_message.astype(F32) * valid).astype(BF16)
    left = dot(band_ref[0], grad_message[:rim, :], (0, 0))
    right = dot(band_ref[1], grad_message[rim:, :], (0, 0))
    low = left[:rim, :].astype(BF16)
    high = right[2 * rim :, :].astype(BF16)
    spill_odd_ref[...] = jnp.where(side == 0, low, high)
    spill_even_ref[...] = jnp.where(side == 0, high, low)
    spread = spread_inner_ref[...] + jnp.concatenate([left[rim:, :], right[: 2 * rim, :]], axis=0)
    spread = spread * valid_ref[...]
    inner_ref[...] = (own_inner_ref[...] + spread[rim : rows - rim, :]).astype(BF16)
    inside = pltpu.make_async_copy(inner_ref, out_ref.at[inner, :], sems.at[3])
    inside.start()
    own = up_ref[...].astype(F32) + dot(grad_pre, w_in_ref[:latent, :], (1, 1))
    own_ref[...] = own + jnp.concatenate([spread[:rim, :], spread[rows - rim :, :]], axis=0)
    for copy in news:
        copy.wait()
    inside.wait()


def even_kernel(valid_ref, own_ref, back_ref, sum_ref):
    rows = valid_ref.shape[0]
    rim = back_ref.shape[0]
    side, _ = place()
    end = 1 - side
    back = back_ref[...].astype(F32) * valid_ref[pl.ds(pl.multiple_of(end * (rows - rim), rim), rim), :]
    sum_ref[...] = (own_ref[pl.ds(pl.multiple_of(end * rim, rim), rim), :] + back).astype(BF16)


def write_pieces(pieces, turns, me, count, grad_in_ref, grad_out_ref, in_ref, out_ref, sems):
    n_in = grad_in_ref.shape[0] // count
    n_out = grad_out_ref.shape[0] // count
    copies = []
    gain = jnp.zeros((1, grad_in_ref.shape[1]), F32)
    for n, (source, turn) in enumerate(zip(pieces, turns)):
        piece = lax.bitwise_xor(me, turn)
        at_in = pl.ds(pl.multiple_of(piece * n_in, n_in), n_in)
        at_out = pl.ds(pl.multiple_of(piece * n_out, n_out), n_out)
        in_ref[n] = source[:n_in, :].astype(F32)
        copies.append(pltpu.make_async_copy(in_ref.at[n], grad_in_ref.at[at_in, :], sems.at[2 * n]))
        copies[-1].start()
        out_ref[n] = source[n_in : n_in + n_out, :].astype(F32)
        copies.append(pltpu.make_async_copy(out_ref.at[n], grad_out_ref.at[at_out, :], sems.at[2 * n + 1]))
        copies[-1].start()
        gain = gain + source[n_in + n_out :, :].astype(F32)[:1, :]
    return gain, copies


def finish_kernel(started_ref, valid_ref, own_ref, even_ref, back_ref, *refs):
    near = refs[:-9]
    out_ref, grad_in_ref, grad_out_ref, gain_ref, held_ref, in_ref, piece_out_ref, sems, piece_sems = refs[-9:]
    rows = valid_ref.shape[0]
    rim = back_ref.shape[0]
    side, me = place()
    at_even = pl.multiple_of((1 - side) * (rows - rim), rim)
    at_odd = pl.multiple_of(side * (rows - rim), rim)
    first = pltpu.make_async_copy(even_ref, out_ref.at[pl.ds(at_even, rim), :], sems.at[0])
    first.start()
    back = back_ref[...].astype(F32) * valid_ref[pl.ds(at_odd, rim), :]
    held_ref[...] = (own_ref[pl.ds(pl.multiple_of(side * rim, rim), rim), :] + back).astype(BF16)
    second = pltpu.make_async_copy(held_ref, out_ref.at[pl.ds(at_odd, rim), :], sems.at[1])
    second.start()
    turns = range(0, 2 * len(near), 2)
    gain_ref[...], copies = write_pieces(
        near, turns, me, 2 * len(near), grad_in_ref, grad_out_ref, in_ref, piece_out_ref, piece_sems
    )
    first.wait()
    second.wait()
    for copy in copies:
        copy.wait()


def unpack_kernel(begun_in_ref, begun_out_ref, gain_near_ref, *refs):
    grad_in_ref, grad_out_ref, gain_ref, in_ref, piece_out_ref, total_ref, sems, gain_sem = refs[-8:]
    far = refs[:-8]
    _, me = place()
    turns = range(1, 2 * len(far), 2)
    gain, copies = write_pieces(
        far, turns, me, 2 * len(far), grad_in_ref, grad_out_ref, in_ref, piece_out_ref, sems
    )
    total_ref[...] = gain_near_ref[...] + gain
    copies.append(pltpu.make_async_copy(total_ref, gain_ref, gain_sem))
    copies[-1].start()
    for copy in copies:
        copy.wait()


def swap(x, axis, turn):
    count = lax.axis_size(axis)
    return lax.ppermute(x, axis, [(i, i ^ turn) for i in range(count)])


def gathered(x, axis):
    count = lax.axis_size(axis)
    if count & (count - 1) == 0:
        return [x] + [swap(x, axis, k) for k in range(1, count)]
    moved = [x] + [
        lax.ppermute(x, axis, [(i, (i + k) % count) for i in range(count)]) for k in range(1, count)
    ]
    order = (lax.axis_index(axis) - jnp.arange(count)) % count
    stacked = jnp.stack(moved)[order]
    return [stacked[k] for k in range(count)]


def tree_sum(parts):
    parts = [part.astype(F32) for part in parts]
    while len(parts) > 1:
        paired = [parts[i] + parts[i + 1] for i in range(0, len(parts) - 1, 2)]
        parts = paired + parts[len(parts) - len(parts) % 2 :]
    return parts[0]


def vmem(count):
    return [pl.BlockSpec(memory_space=pltpu.VMEM)] * count


def shapes(*given):
    return tuple(jax.ShapeDtypeStruct(shape, dtype) for shape, dtype in given)


def kernel(body, name, inputs, outputs, scratch=(), flops=0, moved=0, aliases=None):
    far, arrays = inputs
    spaces = [out.memory_space if hasattr(out, "memory_space") else pltpu.VMEM for out in outputs]
    call = pl.pallas_call(
        body,
        out_shape=outputs,
        in_specs=[pl.BlockSpec(memory_space=pltpu.HBM)] * far + vmem(arrays),
        out_specs=tuple(pl.BlockSpec(memory_space=space) for space in spaces),
        scratch_shapes=list(scratch),
        input_output_aliases=aliases or {},
        compiler_params=pltpu.CompilerParams(vmem_limit_bytes=VMEM_LIMIT),
        cost_estimate=pl.CostEstimate(flops=flops, bytes_accessed=moved, transcendentals=0),
        name=name,
    )

    def run(*given):
        placed = [pltpu.with_memory_space_constraint(x, pltpu.HBM) for x in given[:far]]
        return call(*placed, *given[far:])

    return run


def local(node_state, edge_tiles, block_mask, block_len, w_in, w_out, gain, upstream):
    rows, latent = node_state.shape
    offsets, bs = edge_tiles.shape[1:]
    rim = (offsets - 1) // 2 * bs
    inside = rows - 2 * rim
    width = 3 * rim
    dom = lax.axis_size("dom")
    rep = lax.axis_size("rep")
    total = dom * rep
    scale = 1.0 / math.sqrt(rows * total)
    ring = ("dom", "rep")
    next_pairs = [(i, (i + 1) % total) for i in range(total)]
    back_pairs = [(i, (i - 1) % total) for i in range(total)]
    even_pairs = [(i, i ^ 1) for i in range(total)]
    odd_pairs = [(i, (i + 1) % total if i % 2 else (i - 1) % total) for i in range(total)]
    gain_row = gain.reshape(1, latent)
    tiles = jnp.transpose(edge_tiles, (1, 0, 2))

    to_back, to_next = kernel(
        functools.partial(pack_kernel, bs),
        "pack_rims",
        (2, 0),
        shapes(((rim, latent), BF16), ((rim, latent), BF16)),
        [
            pltpu.VMEM((2, rim, latent), BF16),
            pltpu.SMEM(block_len.shape, jnp.int32),
            pltpu.SemaphoreType.DMA((3,)),
        ],
    )(block_len, node_state)
    from_back = lax.ppermute(to_next, ring, next_pairs)
    from_next = lax.ppermute(to_back, ring, back_pairs)

    work = 2 * inside * latent * (width + 5 * latent + 2 * latent + 2 * latent + width)
    new_inner, own_inner, spread_inner, sum_in, sum_out, sum_gain, band, message, direct, *kept = kernel(
        functools.partial(inner_kernel, (bs, offsets)),
        "inner_rows",
        (8, 0),
        shapes(
            ((inside, latent), BF16),
            ((inside, latent), F32),
            ((rows, latent), F32),
            (w_in.shape, F32),
            (w_out.shape, F32),
            ((1, latent), F32),
            ((2, rim, width), BF16),
            ((2 * rim, latent), F32),
            ((2 * rim, latent), F32),
            ((rows, 1), F32),
            ((2 * rim, latent), BF16),
            ((2 * rim, latent), BF16),
            (w_in.shape, BF16),
            (w_out.shape, BF16),
            ((1, latent), F32),
        ),
        [
            pltpu.SMEM(block_len.shape, jnp.int32),
            pltpu.SMEM(block_mask.shape, jnp.int32),
            pltpu.VMEM((rows, latent), BF16),
            pltpu.VMEM(tiles.shape, BF16),
            pltpu.VMEM((inside, latent), BF16),
            pltpu.VMEM((rows, latent), BF16),
            pltpu.VMEM((inside // rim, rim, width), BF16),
            pltpu.SemaphoreType.DMA((11 + offsets,)),
        ],
        flops=work,
        moved=10 * 1024 * 1024,
    )(block_len, block_mask, node_state, tiles, upstream, w_in, w_out, gain_row)

    n_in, n_out = w_in.shape[0] // dom, w_out.shape[0] // dom
    piece_rows = n_in + n_out + GAIN_ROWS
    send, new_rim, pre_rim = kernel(
        functools.partial(rim_kernel, scale),
        "rim_rows",
        (0, 14),
        shapes(
            ((2, dom // 2, piece_rows, latent), BF16),
            ((2 * rim, latent), BF16),
            ((2 * rim, latent), BF16),
        ),
        [pltpu.VMEM(w_in.shape, F32), pltpu.VMEM(w_out.shape, F32)],
        flops=work,
        moved=8 * 1024 * 1024,
    )(
        *kept,
        band, message, direct, sum_in, sum_out, sum_gain, from_back, from_next,
    )

    valid, _, up_rim, w_in_near, _, _ = kept
    spill_odd, spill_even, own_rim, new_state, grad_state = kernel(
        back_kernel,
        "rim_back",
        (0, 9),
        shapes(((rim, latent), BF16), ((rim, latent), BF16), ((2 * rim, latent), F32))
        + (pltpu.HBM((rows, latent), BF16), pltpu.HBM((rows, latent), BF16)),
        [pltpu.VMEM((inside, latent), BF16), pltpu.SemaphoreType.DMA((4,))],
        flops=2 * inside * latent * (2 * latent + width),
        moved=4 * 1024 * 1024,
    )(valid, up_rim, w_in_near, band, pre_rim, new_inner, new_rim, own_inner, spread_inner)
    back_odd = lax.ppermute(spill_odd, ring, odd_pairs)
    back_even = lax.ppermute(spill_even, ring, even_pairs)
    (even_rows,) = kernel(
        even_kernel,
        "even_rows",
        (0, 3),
        shapes(((rim, latent), BF16)),
    )(valid, own_rim, back_even)
    other = swap(send[1], "dom", 1)
    held = (send[0].astype(F32) + other.astype(F32)).astype(BF16)
    held = [held[k] for k in range(dom // 2)]

    parts = [held[0]] + [swap(held[k], "dom", 2 * k) for k in range(1, dom // 2)]
    quarter = sum(part.astype(F32) for part in parts).astype(BF16)
    planes = gathered(quarter, "rep")
    mine = tree_sum(planes).astype(BF16)
    mine, even_rows = lax.optimization_barrier((mine, even_rows))
    near = [mine] + [swap(mine, "dom", 2 * k) for k in range(1, dom // 2)]
    near[-1], back_odd = lax.optimization_barrier((near[-1], back_odd))
    other = swap(jnp.stack(near), "dom", 1)
    pieces = dom // 2
    piece_scratch = [
        pltpu.VMEM((pieces, n_in, latent), F32),
        pltpu.VMEM((pieces, n_out, latent), F32),
    ]
    sums = (pltpu.HBM(w_in.shape, F32), pltpu.HBM(w_out.shape, F32)) + shapes(((1, latent), F32))
    grad_state, grad_w_in, grad_w_out, gain_near = kernel(
        finish_kernel,
        "finish_state",
        (1, 4 + pieces),
        (pltpu.HBM((rows, latent), BF16),) + sums,
        [pltpu.VMEM((rim, latent), BF16)]
        + piece_scratch
        + [pltpu.SemaphoreType.DMA((2,)), pltpu.SemaphoreType.DMA((2 * pieces,))],
        aliases={0: 0},
    )(grad_state, valid, own_rim, even_rows, back_odd, *near)
    grad_w_in, grad_w_out, grad_gain = kernel(
        unpack_kernel,
        "unpack_sums",
        (2, 1 + pieces),
        sums[:2] + (pltpu.HBM((1, latent), F32),),
        piece_scratch
        + [pltpu.VMEM((1, latent), F32), pltpu.SemaphoreType.DMA((2 * pieces,)), pltpu.SemaphoreType.DMA],
        aliases={0: 0, 1: 1},
    )(grad_w_in, grad_w_out, gain_near, *[other[k] for k in range(pieces)])
    return new_state, grad_state, grad_w_in, grad_w_out, grad_gain.reshape(latent)


def solution(mesh):
    placed = (
        P(("dom", "rep"), None),
        P(("dom", "rep"), None, None),
        P(("dom", "rep"), None),
        P(("dom", "rep")),
        P(),
        P(),
        P(),
        P(("dom", "rep"), None),
    )
    return jax.shard_map(
        local,
        mesh=mesh,
        in_specs=placed,
        out_specs=(P(("dom", "rep"), None), P(("dom", "rep"), None), P(), P(), P()),
        check_vma=False,
    )
```

```python
import functools
import math

import jax
import jax.numpy as jnp
from jax import lax
from jax.experimental import pallas as pl
from jax.experimental.pallas import tpu as pltpu
from jax.sharding import PartitionSpec as P

EPSILON = 1e-05
F32 = jnp.float32
BF16 = jnp.bfloat16
GAIN_ROWS = 8
VMEM_LIMIT = 40 * 1024 * 1024


def dot(a, b, contract):
    return lax.dot_general(a, b, ((contract[:1], contract[1:]), ((), ())), preferred_element_type=F32)


def sublane(bs):
    return lax.broadcasted_iota(jnp.int32, (bs, 1), 0)


def validity(len_ref, first, count, bs):
    return jnp.concatenate(
        [(sublane(bs) < len_ref[first + j]).astype(F32) for j in range(count)], axis=0
    )


def place():
    me = lax.axis_index("dom")
    index = me * lax.axis_size("rep") + lax.axis_index("rep")
    return lax.rem(index, 2), me


def pack_kernel(bs, len_ref, state_ref, first_ref, last_ref, held_ref, lens_ref, sems):
    rows = state_ref.shape[0]
    rim = first_ref.shape[0]
    per = rim // bs
    copies = [
        pltpu.make_async_copy(len_ref, lens_ref, sems.at[0]),
        pltpu.make_async_copy(state_ref.at[pl.ds(rows - rim, rim), :], held_ref.at[1], sems.at[1]),
        pltpu.make_async_copy(state_ref.at[pl.ds(0, rim), :], held_ref.at[0], sems.at[2]),
    ]
    for copy in copies:
        copy.start()
    for copy in copies:
        copy.wait()
    blocks = rows // bs
    for j in range(per):
        here = slice(j * bs, (j + 1) * bs)
        first_ref[here, :] = held_ref[0, here, :] * (sublane(bs) < lens_ref[j]).astype(F32).astype(BF16)
        last_ref[here, :] = held_ref[1, here, :] * (
            sublane(bs) < lens_ref[blocks - per + j]
        ).astype(F32).astype(BF16)


def fill_band(band_ref, tiles_ref, mask_ref, first, per, bs, offsets):
    for j in range(per):
        row = slice(j * bs, (j + 1) * bs)
        for column in range(per + offsets - 1):
            offset = column - j
            cols = slice(column * bs, (column + 1) * bs)
            if 0 <= offset < offsets:
                tile = tiles_ref[offset, (first + j) * bs : (first + j + 1) * bs, :]
                band_ref[row, cols] = tile * mask_ref[first + j, offset].astype(F32).astype(BF16)
            else:
                band_ref[row, cols] = jnp.zeros((bs, bs), BF16)


def node_rows(state, message, direct_part, upstream, valid, w_in_ref, w_out_ref, gain):
    latent = state.shape[1]
    preact = direct_part + dot(message, w_in_ref[latent:, :], (1, 0))
    sigma = jax.nn.sigmoid(preact)
    activated = (preact * sigma).astype(BF16)
    output = dot(activated, w_out_ref[...], (1, 0))
    centred = output - jnp.mean(output, axis=1, keepdims=True)
    inverse = lax.rsqrt(jnp.mean(centred * centred, axis=1, keepdims=True) + EPSILON)
    normed = centred * inverse
    new_state = (state.astype(F32) + gain * normed * valid).astype(BF16)
    masked_up = upstream * valid
    gain_sum = jnp.sum(masked_up * normed, axis=0, keepdims=True)
    scaled = masked_up * gain
    grad_output = (
        inverse
        * (
            scaled
            - jnp.mean(scaled, axis=1, keepdims=True)
            - normed * jnp.mean(scaled * normed, axis=1, keepdims=True)
        )
    ).astype(BF16)
    grad_act = dot(grad_output, w_out_ref[...], (1, 1))
    slope = sigma * (1.0 + preact * (1.0 - sigma))
    grad_pre = (grad_act * slope).astype(BF16)
    return new_state, gain_sum, activated, grad_output, grad_pre


def inner_kernel(
    cfg,
    len_hbm,
    mask_hbm,
    state_hbm,
    tiles_hbm,
    up_hbm,
    w_in_hbm,
    w_out_hbm,
    gain_hbm,
    new_ref,
    own_ref,
    spread_ref,
    grad_in_ref,
    grad_out_ref,
    gain_sum_ref,
    rim_band_ref,
    rim_message_ref,
    rim_direct_ref,
    valid_ref,
    state_rim_ref,
    up_rim_ref,
    w_in_ref,
    w_out_ref,
    gain_ref,
    len_ref,
    mask_ref,
    state_ref,
    tiles_ref,
    up_ref,
    ext_ref,
    band_ref,
    sems,
):
    bs, offsets = cfg
    rim = (offsets - 1) // 2 * bs
    rows, latent = state_ref.shape
    per = rim // bs
    blocks = rows // bs
    width = 3 * rim
    low, inner, high = pl.ds(0, rim), pl.ds(rim, rows - 2 * rim), pl.ds(rows - rim, rim)
    late = pl.ds(rim, rim)

    pairs = [(len_hbm, len_ref), (mask_hbm, mask_ref), (state_hbm, state_ref)]
    pairs += [(tiles_hbm.at[o], tiles_ref.at[o]) for o in range(offsets)]
    first = len(pairs)
    pairs += [(w_in_hbm, w_in_ref), (w_out_hbm, w_out_ref), (gain_hbm, gain_ref)]
    pairs += [(up_hbm.at[inner, :], up_ref)]
    second = len(pairs)
    pairs += [(state_hbm.at[low, :], state_rim_ref.at[low, :]), (state_hbm.at[high, :], state_rim_ref.at[late, :])]
    pairs += [(up_hbm.at[low, :], up_rim_ref.at[low, :]), (up_hbm.at[high, :], up_rim_ref.at[late, :])]
    copies = [pltpu.make_async_copy(a, b, sems.at[i]) for i, (a, b) in enumerate(pairs)]
    for copy in copies:
        copy.start()
    for copy in copies[:first]:
        copy.wait()

    valid_ref[...] = validity(len_ref, 0, blocks, bs)
    ext_ref[...] = (state_ref[...].astype(F32) * valid_ref[...]).astype(BF16)
    message = []
    for chunk in range(1, rows // rim - 1):
        band = band_ref.at[chunk - 1]
        fill_band(band, tiles_ref, mask_ref, chunk * per, per, bs, offsets)
        message.append(dot(band[...], ext_ref[(chunk - 1) * rim : (chunk - 1) * rim + width, :], (1, 0)))
    inner = slice(rim, rows - rim)
    valid = valid_ref[inner, :]
    message = (jnp.concatenate(message, axis=0) * valid).astype(BF16)
    for copy in copies[first:second]:
        copy.wait()
    state = state_ref[inner, :]
    upstream = up_ref[...].astype(F32)
    direct_part = dot(state, w_in_ref[:latent, :], (1, 0))
    new_state, gain_sum, activated, grad_output, grad_pre = node_rows(
        state, message, direct_part, upstream, valid, w_in_ref, w_out_ref, gain_ref[...]
    )
    new_ref[...] = new_state
    gain_sum_ref[...] = gain_sum
    grad_out_ref[...] = dot(activated, grad_output, (0, 0))
    grad_in_ref[:latent, :] = dot(state, grad_pre, (0, 0))
    grad_in_ref[latent:, :] = dot(message, grad_pre, (0, 0))
    own_ref[...] = upstream + dot(grad_pre, w_in_ref[:latent, :], (1, 1))
    grad_message = dot(grad_pre, w_in_ref[latent:, :], (1, 1)).astype(BF16)
    grad_message = (grad_message.astype(F32) * valid).astype(BF16)
    spread_ref[...] = jnp.zeros_like(spread_ref)
    for chunk in range(1, rows // rim - 1):
        reach = slice((chunk - 1) * rim, (chunk - 1) * rim + width)
        spread_ref[reach, :] += dot(
            band_ref[chunk - 1], grad_message[(chunk - 1) * rim : chunk * rim, :], (0, 0)
        )

    for end in range(2):
        first = end * (blocks - per)
        band = rim_band_ref.at[end]
        fill_band(band, tiles_ref, mask_ref, first, per, bs, offsets)
        here = slice(end * rim, (end + 1) * rim)
        if end == 0:
            rim_message_ref[here, :] = dot(band[:, rim:], ext_ref[: 2 * rim, :], (1, 0))
        else:
            rim_message_ref[here, :] = dot(band[:, : 2 * rim], ext_ref[rows - 2 * rim :, :], (1, 0))
        rim_direct_ref[here, :] = dot(
            state_ref[first * bs : first * bs + rim, :], w_in_ref[:latent, :], (1, 0)
        )
    for copy in copies[second:]:
        copy.wait()


def rim_kernel(
    scale,
    valid_ref,
    state_ref,
    up_ref,
    w_in_ref,
    w_out_ref,
    gain_ref,
    band_ref,
    message_ref,
    direct_ref,
    inner_in_ref,
    inner_out_ref,
    inner_gain_ref,
    low_ref,
    high_ref,
    keep_ref,
    give_ref,
    new_ref,
    pre_ref,
    grad_in_ref,
    grad_out_ref,
):
    rows = valid_ref.shape[0]
    rim, latent = low_ref.shape
    _, me = place()
    valid = jnp.concatenate([valid_ref[:rim, :], valid_ref[rows - rim :, :]], axis=0)
    arrived = jnp.concatenate(
        [dot(band_ref[0, :, :rim], low_ref[...], (1, 0)), dot(band_ref[1, :, 2 * rim :], high_ref[...], (1, 0))], axis=0
    )
    message = ((message_ref[...] + arrived) * valid).astype(BF16)
    state = state_ref[...]
    upstream = up_ref[...].astype(F32)
    new_state, gain_sum, activated, grad_output, grad_pre = node_rows(
        state, message, direct_ref[...], upstream, valid, w_in_ref, w_out_ref, gain_ref[...]
    )
    new_ref[...] = new_state
    gain_sum = gain_sum + inner_gain_ref[...]
    grad_out_ref[...] = inner_out_ref[...] + dot(activated, grad_output, (0, 0))
    grad_in_ref[:latent, :] = inner_in_ref[:latent, :] + dot(state, grad_pre, (0, 0))
    grad_in_ref[latent:, :] = inner_in_ref[latent:, :] + dot(message, grad_pre, (0, 0))
    pre_ref[...] = grad_pre

    count = 2 * keep_ref.shape[0]
    n_in = grad_in_ref.shape[0] // count
    n_out = grad_out_ref.shape[0] // count
    top = lax.broadcasted_iota(jnp.int32, (GAIN_ROWS, latent), 0) == 0
    gain_rows = jnp.where(top, gain_sum * scale, 0.0)
    for turn in range(count):
        piece = lax.bitwise_xor(me, turn)
        target = (give_ref if turn % 2 else keep_ref).at[turn // 2]
        at_in = pl.ds(pl.multiple_of(piece * n_in, n_in), n_in)
        at_out = pl.ds(pl.multiple_of(piece * n_out, n_out), n_out)
        target[:n_in, :] = (grad_in_ref[at_in, :] * scale).astype(BF16)
        target[n_in : n_in + n_out, :] = (grad_out_ref[at_out, :] * scale).astype(BF16)
        target[n_in + n_out :, :] = jnp.where(piece == 0, gain_rows, 0.0).astype(BF16)


def back_kernel(
    valid_ref,
    up_ref,
    w_in_ref,
    band_ref,
    pre_ref,
    new_inner_ref,
    new_rim_ref,
    own_inner_ref,
    spread_inner_ref,
    spill_odd_ref,
    spill_even_ref,
    own_ref,
    new_ref,
    out_ref,
    inner_ref,
    sems,
):
    rim, latent = spill_odd_ref.shape
    rows = valid_ref.shape[0]
    side, _ = place()
    inner = pl.ds(rim, rows - 2 * rim)
    news = [
        pltpu.make_async_copy(new_rim_ref.at[pl.ds(0, rim), :], new_ref.at[pl.ds(0, rim), :], sems.at[0]),
        pltpu.make_async_copy(new_inner_ref, new_ref.at[inner, :], sems.at[1]),
        pltpu.make_async_copy(
            new_rim_ref.at[pl.ds(rim, rim), :], new_ref.at[pl.ds(rows - rim, rim), :], sems.at[2]
        ),
    ]
    for copy in news:
        copy.start()
    valid = jnp.concatenate([valid_ref[:rim, :], valid_ref[rows - rim :, :]], axis=0)
    grad_pre = pre_ref[...]
    grad_message = dot(grad_pre, w_in_ref[latent:, :], (1, 1)).astype(BF16)
    grad_message = (grad_message.astype(F32) * valid).astype(BF16)
    left = dot(band_ref[0], grad_message[:rim, :], (0, 0))
    right = dot(band_ref[1], grad_message[rim:, :], (0, 0))
    low = left[:rim, :].astype(BF16)
    high = right[2 * rim :, :].astype(BF16)
    spill_odd_ref[...] = jnp.where(side == 0, low, high)
    spill_even_ref[...] = jnp.where(side == 0, high, low)
    spread = spread_inner_ref[...] + jnp.concatenate([left[rim:, :], right[: 2 * rim, :]], axis=0)
    spread = spread * valid_ref[...]
    inner_ref[...] = (own_inner_ref[...] + spread[rim : rows - rim, :]).astype(BF16)
    inside = pltpu.make_async_copy(inner_ref, out_ref.at[inner, :], sems.at[3])
    inside.start()
    own = up_ref[...].astype(F32) + dot(grad_pre, w_in_ref[:latent, :], (1, 1))
    own_ref[...] = own + jnp.concatenate([spread[:rim, :], spread[rows - rim :, :]], axis=0)
    for copy in news:
        copy.wait()
    inside.wait()


def even_kernel(valid_ref, own_ref, back_ref, sum_ref):
    rows = valid_ref.shape[0]
    rim = back_ref.shape[0]
    side, _ = place()
    end = 1 - side
    back = back_ref[...].astype(F32) * valid_ref[pl.ds(pl.multiple_of(end * (rows - rim), rim), rim), :]
    sum_ref[...] = (own_ref[pl.ds(pl.multiple_of(end * rim, rim), rim), :] + back).astype(BF16)


def write_pieces(pieces, turns, me, count, grad_in_ref, grad_out_ref, in_ref, out_ref, sems):
    n_in = grad_in_ref.shape[0] // count
    n_out = grad_out_ref.shape[0] // count
    copies = []
    gain = jnp.zeros((1, grad_in_ref.shape[1]), F32)
    for n, (source, turn) in enumerate(zip(pieces, turns)):
        piece = lax.bitwise_xor(me, turn)
        at_in = pl.ds(pl.multiple_of(piece * n_in, n_in), n_in)
        at_out = pl.ds(pl.multiple_of(piece * n_out, n_out), n_out)
        in_ref[n] = source[:n_in, :].astype(F32)
        copies.append(pltpu.make_async_copy(in_ref.at[n], grad_in_ref.at[at_in, :], sems.at[2 * n]))
        copies[-1].start()
        out_ref[n] = source[n_in : n_in + n_out, :].astype(F32)
        copies.append(pltpu.make_async_copy(out_ref.at[n], grad_out_ref.at[at_out, :], sems.at[2 * n + 1]))
        copies[-1].start()
        gain = gain + source[n_in + n_out :, :].astype(F32)[:1, :]
    return gain, copies


def finish_kernel(started_ref, valid_ref, own_ref, even_ref, back_ref, *refs):
    near = refs[:-9]
    out_ref, grad_in_ref, grad_out_ref, gain_ref, held_ref, in_ref, piece_out_ref, sems, piece_sems = refs[-9:]
    rows = valid_ref.shape[0]
    rim = back_ref.shape[0]
    side, me = place()
    at_even = pl.multiple_of((1 - side) * (rows - rim), rim)
    at_odd = pl.multiple_of(side * (rows - rim), rim)
    first = pltpu.make_async_copy(even_ref, out_ref.at[pl.ds(at_even, rim), :], sems.at[0])
    first.start()
    back = back_ref[...].astype(F32) * valid_ref[pl.ds(at_odd, rim), :]
    held_ref[...] = (own_ref[pl.ds(pl.multiple_of(side * rim, rim), rim), :] + back).astype(BF16)
    second = pltpu.make_async_copy(held_ref, out_ref.at[pl.ds(at_odd, rim), :], sems.at[1])
    second.start()
    turns = range(0, 2 * len(near), 2)
    gain_ref[...], copies = write_pieces(
        near, turns, me, 2 * len(near), grad_in_ref, grad_out_ref, in_ref, piece_out_ref, piece_sems
    )
    first.wait()
    second.wait()
    for copy in copies:
        copy.wait()


def unpack_kernel(begun_in_ref, begun_out_ref, gain_near_ref, *refs):
    grad_in_ref, grad_out_ref, gain_ref, in_ref, piece_out_ref, total_ref, sems, gain_sem = refs[-8:]
    far = [refs[0].at[n] for n in range(refs[0].shape[0])]
    _, me = place()
    turns = range(1, 2 * len(far), 2)
    gain, copies = write_pieces(
        far, turns, me, 2 * len(far), grad_in_ref, grad_out_ref, in_ref, piece_out_ref, sems
    )
    total_ref[...] = gain_near_ref[...] + gain
    copies.append(pltpu.make_async_copy(total_ref, gain_ref, gain_sem))
    copies[-1].start()
    for copy in copies:
        copy.wait()


def swap(x, axis, turn):
    count = lax.axis_size(axis)
    return lax.ppermute(x, axis, [(i, i ^ turn) for i in range(count)])


def gathered(x, axis):
    count = lax.axis_size(axis)
    if count & (count - 1) == 0:
        return [x] + [swap(x, axis, k) for k in range(1, count)]
    moved = [x] + [
        lax.ppermute(x, axis, [(i, (i + k) % count) for i in range(count)]) for k in range(1, count)
    ]
    order = (lax.axis_index(axis) - jnp.arange(count)) % count
    stacked = jnp.stack(moved)[order]
    return [stacked[k] for k in range(count)]


def tree_sum(parts):
    parts = [part.astype(F32) for part in parts]
    while len(parts) > 1:
        paired = [parts[i] + parts[i + 1] for i in range(0, len(parts) - 1, 2)]
        parts = paired + parts[len(parts) - len(parts) % 2 :]
    return parts[0]


def vmem(count):
    return [pl.BlockSpec(memory_space=pltpu.VMEM)] * count


def shapes(*given):
    return tuple(jax.ShapeDtypeStruct(shape, dtype) for shape, dtype in given)


def kernel(body, name, inputs, outputs, scratch=(), flops=0, moved=0, aliases=None):
    far, arrays = inputs
    spaces = [out.memory_space if hasattr(out, "memory_space") else pltpu.VMEM for out in outputs]
    call = pl.pallas_call(
        body,
        out_shape=outputs,
        in_specs=[pl.BlockSpec(memory_space=pltpu.HBM)] * far + vmem(arrays),
        out_specs=tuple(pl.BlockSpec(memory_space=space) for space in spaces),
        scratch_shapes=list(scratch),
        input_output_aliases=aliases or {},
        compiler_params=pltpu.CompilerParams(vmem_limit_bytes=VMEM_LIMIT),
        cost_estimate=pl.CostEstimate(flops=flops, bytes_accessed=moved, transcendentals=0),
        name=name,
    )

    def run(*given):
        placed = [pltpu.with_memory_space_constraint(x, pltpu.HBM) for x in given[:far]]
        return call(*placed, *given[far:])

    return run


def local(node_state, edge_tiles, block_mask, block_len, w_in, w_out, gain, upstream):
    rows, latent = node_state.shape
    offsets, bs = edge_tiles.shape[1:]
    rim = (offsets - 1) // 2 * bs
    inside = rows - 2 * rim
    width = 3 * rim
    dom = lax.axis_size("dom")
    rep = lax.axis_size("rep")
    total = dom * rep
    scale = 1.0 / math.sqrt(rows * total)
    ring = ("dom", "rep")
    next_pairs = [(i, (i + 1) % total) for i in range(total)]
    back_pairs = [(i, (i - 1) % total) for i in range(total)]
    even_pairs = [(i, i ^ 1) for i in range(total)]
    odd_pairs = [(i, (i + 1) % total if i % 2 else (i - 1) % total) for i in range(total)]
    gain_row = gain.reshape(1, latent)
    tiles = jnp.transpose(edge_tiles, (1, 0, 2))

    to_back, to_next = kernel(
        functools.partial(pack_kernel, bs),
        "pack_rims",
        (2, 0),
        shapes(((rim, latent), BF16), ((rim, latent), BF16)),
        [
            pltpu.VMEM((2, rim, latent), BF16),
            pltpu.SMEM(block_len.shape, jnp.int32),
            pltpu.SemaphoreType.DMA((3,)),
        ],
    )(block_len, node_state)
    from_back = lax.ppermute(to_next, ring, next_pairs)
    from_next = lax.ppermute(to_back, ring, back_pairs)

    work = 2 * inside * latent * (width + 5 * latent + 2 * latent + 2 * latent + width)
    new_inner, own_inner, spread_inner, sum_in, sum_out, sum_gain, band, message, direct, *kept = kernel(
        functools.partial(inner_kernel, (bs, offsets)),
        "inner_rows",
        (8, 0),
        shapes(
            ((inside, latent), BF16),
            ((inside, latent), F32),
            ((rows, latent), F32),
            (w_in.shape, F32),
            (w_out.shape, F32),
            ((1, latent), F32),
            ((2, rim, width), BF16),
            ((2 * rim, latent), F32),
            ((2 * rim, latent), F32),
            ((rows, 1), F32),
            ((2 * rim, latent), BF16),
            ((2 * rim, latent), BF16),
            (w_in.shape, BF16),
            (w_out.shape, BF16),
            ((1, latent), F32),
        ),
        [
            pltpu.SMEM(block_len.shape, jnp.int32),
            pltpu.SMEM(block_mask.shape, jnp.int32),
            pltpu.VMEM((rows, latent), BF16),
            pltpu.VMEM(tiles.shape, BF16),
            pltpu.VMEM((inside, latent), BF16),
            pltpu.VMEM((rows, latent), BF16),
            pltpu.VMEM((inside // rim, rim, width), BF16),
            pltpu.SemaphoreType.DMA((11 + offsets,)),
        ],
        flops=work,
        moved=10 * 1024 * 1024,
    )(block_len, block_mask, node_state, tiles, upstream, w_in, w_out, gain_row)

    n_in, n_out = w_in.shape[0] // dom, w_out.shape[0] // dom
    piece_rows = n_in + n_out + GAIN_ROWS
    keep, give, new_rim, pre_rim = kernel(
        functools.partial(rim_kernel, scale),
        "rim_rows",
        (0, 14),
        shapes(
            ((dom // 2, piece_rows, latent), BF16),
            ((dom // 2, piece_rows, latent), BF16),
            ((2 * rim, latent), BF16),
            ((2 * rim, latent), BF16),
        ),
        [pltpu.VMEM(w_in.shape, F32), pltpu.VMEM(w_out.shape, F32)],
        flops=work,
        moved=8 * 1024 * 1024,
    )(
        *kept,
        band, message, direct, sum_in, sum_out, sum_gain, from_back, from_next,
    )

    valid, _, up_rim, w_in_near, _, _ = kept
    spill_odd, spill_even, own_rim, new_state, grad_state = kernel(
        back_kernel,
        "rim_back",
        (0, 9),
        shapes(((rim, latent), BF16), ((rim, latent), BF16), ((2 * rim, latent), F32))
        + (pltpu.HBM((rows, latent), BF16), pltpu.HBM((rows, latent), BF16)),
        [pltpu.VMEM((inside, latent), BF16), pltpu.SemaphoreType.DMA((4,))],
        flops=2 * inside * latent * (2 * latent + width),
        moved=4 * 1024 * 1024,
    )(valid, up_rim, w_in_near, band, pre_rim, new_inner, new_rim, own_inner, spread_inner)
    back_odd = lax.ppermute(spill_odd, ring, odd_pairs)
    back_even = lax.ppermute(spill_even, ring, even_pairs)
    (even_rows,) = kernel(
        even_kernel,
        "even_rows",
        (0, 3),
        shapes(((rim, latent), BF16)),
    )(valid, own_rim, back_even)
    other = swap(give, "dom", 1)
    held = (keep.astype(F32) + other.astype(F32)).astype(BF16)
    held = [held[k] for k in range(dom // 2)]

    parts = [held[0]] + [swap(held[k], "dom", 2 * k) for k in range(1, dom // 2)]
    quarter = sum(part.astype(F32) for part in parts).astype(BF16)
    planes = gathered(quarter, "rep")
    mine = tree_sum(planes).astype(BF16)
    mine, even_rows = lax.optimization_barrier((mine, even_rows))
    near = [mine] + [swap(mine, "dom", 2 * k) for k in range(1, dom // 2)]
    near[-1], back_odd = lax.optimization_barrier((near[-1], back_odd))
    other = swap(jnp.stack(near), "dom", 1)
    pieces = dom // 2
    piece_scratch = [
        pltpu.VMEM((pieces, n_in, latent), F32),
        pltpu.VMEM((pieces, n_out, latent), F32),
    ]
    sums = (pltpu.HBM(w_in.shape, F32), pltpu.HBM(w_out.shape, F32)) + shapes(((1, latent), F32))
    grad_state, grad_w_in, grad_w_out, gain_near = kernel(
        finish_kernel,
        "finish_state",
        (1, 4 + pieces),
        (pltpu.HBM((rows, latent), BF16),) + sums,
        [pltpu.VMEM((rim, latent), BF16)]
        + piece_scratch
        + [pltpu.SemaphoreType.DMA((2,)), pltpu.SemaphoreType.DMA((2 * pieces,))],
        aliases={0: 0},
    )(grad_state, valid, own_rim, even_rows, back_odd, *near)
    grad_w_in, grad_w_out, grad_gain = kernel(
        unpack_kernel,
        "unpack_sums",
        (2, 2),
        sums[:2] + (pltpu.HBM((1, latent), F32),),
        piece_scratch
        + [pltpu.VMEM((1, latent), F32), pltpu.SemaphoreType.DMA((2 * pieces,)), pltpu.SemaphoreType.DMA],
        aliases={0: 0, 1: 1},
    )(grad_w_in, grad_w_out, gain_near, other)
    return new_state, grad_state, grad_w_in, grad_w_out, grad_gain.reshape(latent)


def solution(mesh):
    placed = (
        P(("dom", "rep"), None),
        P(("dom", "rep"), None, None),
        P(("dom", "rep"), None),
        P(("dom", "rep")),
        P(),
        P(),
        P(),
        P(("dom", "rep"), None),
    )
    return jax.shard_map(
        local,
        mesh=mesh,
        in_specs=placed,
        out_specs=(P(("dom", "rep"), None), P(("dom", "rep"), None), P(), P(), P()),
        check_vma=False,
    )
```
